256 devices in a mesh: dp: 32 (over y, x, z_lo), col: 8 (over z_hi, core).
Axes of the slice: x: 4, y: 4, z: 8 (z_hi: 4, z_lo: 2; z = z_hi * 2 + z_lo), core: 2. Of those that a mesh axis runs over, the one named last changes fastest.
Arguments:
- features: bfloat16 [512, 512, 256], P('dp', 'col'), may hold values from -6 to 6
- cotangent: bfloat16 [512, 512, 256], P('dp'), may hold values from -6 to 6
- lengths: int32 [512], P('dp'), may hold values from 1 to 256, as said below
- route: int32 [512, 2], P('dp'), may hold values from 0 to 31, as said below
- w_in: bfloat16 [4, 512, 512], P(None, None, 'col'), may hold values from -0.25 to 0.25
- w_out: bfloat16 [512, 512], P('col'), may hold values from -0.25 to 0.25
Outputs:
- mixed: bfloat16 [512, 512, 256], P('dp', 'col')
- grad_features: bfloat16 [512, 512, 256], P('dp', 'col')
- grad_in: float32 [4, 512, 512], P(None, None, 'col')
- grad_out: float32 [512, 512], P('col')
The draws below stay inside these ranges and needn't reach their ends.
Inputs may be any that keep to these rules, and one draw needn't show every extreme that they name: `lengths`: positions at or past a history's length are padding; some history has length 256. route[h, 0] is the data group that receives history h and route[h, 1] its slot there; every group receives exactly 16 histories, one in each slot, and the histories of one group go to 16 different groups.
All inputs are finite; a program needn't handle non-finite values.
Results may differ from the reference program's by a relative error of at most 0.039.
Values may be sent and summed in bfloat16 or wider, within the bound.
No kernel may reach another device: no remote copies, remote signals or barrier semaphores. Data moves between devices by JAX's collectives and lax.ppermute only.
A program may use at most 128 MiB of HBM per device.

```python
import jax
import jax.numpy as jnp
from jax import lax

D = 512
H = 8
DH = 64
SLOT = 256
HIST_DEV = 16
HISTS = 512
TOKENS = 131072
N_DP = 32
N_COL = 8


def draw_lengths(key, part):
    key = jax.random.fold_in(key, 5)
    reach_key, length_key = jax.random.split(key)
    levels = jax.random.randint(reach_key, (N_DP, 1), 0, 3)
    reaches = jnp.where(levels == 0, SLOT, jnp.where(levels == 1, SLOT // 2, SLOT // 4))
    raw_draw = jax.random.randint(length_key, (N_DP, HIST_DEV), 0, SLOT)
    drawn_len = raw_draw % reaches + 1
    drawn_len = drawn_len.at[0, 0].set(SLOT)
    return drawn_len.reshape(N_DP * HIST_DEV).astype(jnp.int32)


def slot_order(one_key):
    return jax.random.permutation(one_key, HIST_DEV)


def draw_route(key, part):
    key = jax.random.fold_in(key, 7)
    label_key, offset_key, order_key = jax.random.split(key, 3)
    relabel = jax.random.permutation(label_key, N_DP).astype(jnp.int32)
    position = jnp.zeros((N_DP,), jnp.int32).at[relabel].set(jnp.arange(N_DP, dtype=jnp.int32))
    offsets = jax.random.permutation(offset_key, N_DP).astype(jnp.int32)[:HIST_DEV]
    orders = jax.vmap(slot_order)(jax.random.split(order_key, N_DP)).astype(jnp.int32)
    devices = jnp.arange(N_DP, dtype=jnp.int32)[:, None]
    targets = relabel[(position[devices] + offsets[orders]) % N_DP]
    return jnp.stack([targets, orders], axis=-1).reshape(N_DP * HIST_DEV, 2).astype(jnp.int32)


def block_levels(stream_key, dims, shards, smallest, top_value):
    factor_of, own = 1.0, jax.random.fold_in(stream_key, 6)
    for axis_at, parts in shards:
        steps = jnp.exp(jax.random.uniform(jax.random.fold_in(own, axis_at), (parts,), jnp.float32, smallest / len(shards), top_value / len(shards)))
        factor_of = factor_of * jnp.repeat(steps, dims[axis_at] // parts).reshape([-1 if axis == axis_at else 1 for axis in range(len(dims))])
    return factor_of


def scatter_about(rng, shape, scale, most, cuts=(), kind=jnp.bfloat16):
    result = scale * jax.random.normal(rng, shape, jnp.float32)
    if cuts:
        result = result * block_levels(rng, shape, cuts, -0.22, 0.18)
    return jnp.clip(result, -most, most).astype(kind)


def setup_inputs(seed: int = 0) -> dict:
    key_list = jax.random.split(jax.random.key(seed), 7)
    return {
        "features": scatter_about(key_list[0], (HISTS, D, SLOT), 1.0, 6.0, ((0, 32), (1, 8))),
        "cotangent": scatter_about(key_list[1], (HISTS, D, SLOT), 1.0, 6.0, ((0, 32),)),
        "lengths": draw_lengths(jax.random.fold_in(key_list[6], 71), 0),
        "route": draw_route(jax.random.fold_in(key_list[6], 71), 0),
        "w_in": scatter_about(key_list[4], (4, D, H * DH), D ** -0.5, 0.25, ((2, 8),)),
        "w_out": scatter_about(key_list[5], (H * DH, D), (H * DH) ** -0.5, 0.25, ((0, 8),)),
    }


norm_eps = 1e-05

def silu_slope(values):
    sigma = jax.nn.sigmoid(values)
    return sigma * (1.0 + values * (1.0 - sigma))

def row_norm(values):
    centred = values - lax.optimization_barrier(jnp.mean(values, axis=-1, keepdims=True))
    inv_scale = lax.rsqrt(lax.optimization_barrier(jnp.mean(centred * centred, axis=-1, keepdims=True)) + norm_eps)
    return (centred * inv_scale, inv_scale)

def head_norm(values):
    row_mean = lax.optimization_barrier(jnp.mean(values, axis=-1, keepdims=True))
    spread = lax.optimization_barrier(jnp.mean(values * values, axis=-1, keepdims=True)) - row_mean * row_mean
    inv_scale = lax.rsqrt(spread + norm_eps)
    return ((values - row_mean) * inv_scale, inv_scale)

def norm_back(grads, normed, inv_scale):
    first_mean = lax.optimization_barrier(jnp.mean(grads, axis=-1, keepdims=True))
    second_mean = lax.optimization_barrier(jnp.mean(grads * normed, axis=-1, keepdims=True))
    return inv_scale * (grads - first_mean - normed * second_mean)

def rounded(values):
    return lax.optimization_barrier(values.astype(jnp.bfloat16)).astype(jnp.float32)

def pair_live(length):
    position = jnp.arange(SLOT, dtype=jnp.int32)
    return (position[None, :] <= position[:, None]) & (position[:, None] < length) & (position[None, :] < length)

def history_pass(features, grad_rows, length, w_in, w_out):
    as_float = features.astype(jnp.float32).T
    normed, inv_in = row_norm(as_float)
    normed_bf = normed.astype(jnp.bfloat16).astype(jnp.float32)
    w_float = w_in.astype(jnp.float32)
    wout_float = w_out.astype(jnp.float32)
    pre_act = jnp.einsum('sd,cdf->csf', normed_bf, w_float)
    proj = jax.nn.silu(pre_act).astype(jnp.bfloat16).astype(jnp.float32)
    up_proj = proj[0]
    values = proj[1].reshape(SLOT, H, DH)
    queries = proj[2].reshape(SLOT, H, DH)
    keys = proj[3].reshape(SLOT, H, DH)
    factor = DH ** (-0.5)
    scores = jnp.einsum('ihd,jhd->hij', queries, keys) * factor
    live = pair_live(length)[None]
    weights = rounded(jnp.where(live, jax.nn.silu(scores), 0.0))
    attended = jnp.einsum('hij,jhd->ihd', weights, values).reshape(SLOT, H * DH)
    out_norm, inv_out = head_norm(attended)
    gated = rounded(out_norm * up_proj)
    group_cols = H * DH // N_COL
    totals = as_float
    for group in range(N_COL):
        low = group * group_cols
        term = jnp.dot(gated[:, low:low + group_cols], wout_float[low:low + group_cols], preferred_element_type=jnp.float32)
        totals = totals + rounded(term)
    mixed_rows = totals.astype(jnp.bfloat16)
    grad_float = grad_rows.astype(jnp.float32).T
    grad_gated = jnp.dot(grad_float, wout_float.T, preferred_element_type=jnp.float32)
    grad_wout = jnp.dot(gated.T, grad_float, preferred_element_type=jnp.float32)
    grad_normo = grad_gated * up_proj
    grad_up = grad_gated * out_norm
    grad_att = rounded(norm_back(grad_normo, out_norm, inv_out)).reshape(SLOT, H, DH)
    grad_weights = jnp.einsum('ihd,jhd->hij', grad_att, values)
    grad_values = jnp.einsum('hij,ihd->jhd', weights, grad_att)
    grad_scores = rounded(jnp.where(live, grad_weights * silu_slope(scores), 0.0))
    grad_queries = jnp.einsum('hij,jhd->ihd', grad_scores, keys) * factor
    grad_keys = jnp.einsum('hij,ihd->jhd', grad_scores, queries) * factor
    grad_proj = jnp.stack([grad_up, grad_values.reshape(SLOT, H * DH), grad_queries.reshape(SLOT, H * DH), grad_keys.reshape(SLOT, H * DH)])
    grad_pre = rounded(grad_proj * silu_slope(pre_act))
    grad_win = jnp.einsum('sd,csf->cdf', normed_bf, grad_pre)
    grad_xn = jnp.zeros((SLOT, D), jnp.float32)
    for group in range(N_COL):
        low = group * group_cols
        term = jnp.einsum('csf,cdf->sd', grad_pre[:, :, low:low + group_cols], w_float[:, :, low:low + group_cols])
        grad_xn = grad_xn + rounded(term)
    grad_rows_out = (grad_float + norm_back(grad_xn, normed, inv_in)).astype(jnp.bfloat16)
    return (mixed_rows.T, grad_rows_out.T, grad_win, grad_wout)

def reference(features, cotangent, lengths, route, w_in, w_out):
    target = (route[:, 0] * HIST_DEV + route[:, 1]).astype(jnp.int32)
    back_index = jnp.zeros((HISTS,), jnp.int32).at[target].set(jnp.arange(HISTS, dtype=jnp.int32))
    grad_home = jnp.take(cotangent, target, axis=0)

    def step(carry, entries):
        rows, grad_rows, length = entries
        mixed_rows, grad_rows_out, grad_win, grad_wout = history_pass(rows, grad_rows, length, w_in, w_out)
        return ((carry[0] + grad_win, carry[1] + grad_wout), (mixed_rows, grad_rows_out))
    start_sums = (jnp.zeros((4, D, H * DH), jnp.float32), jnp.zeros((H * DH, D), jnp.float32))
    sums, outputs = lax.scan(step, start_sums, (features, grad_home, lengths))
    factor = float(TOKENS) ** (-0.5)
    mixed = jnp.take(outputs[0], back_index, axis=0)
    return (mixed, outputs[1], sums[0] * factor, sums[1] * factor)
```

```python
import jax
import jax.numpy as jnp
from jax import lax
from jax.experimental import pallas as pl
from jax.experimental.pallas import tpu as pltpu
from jax.sharding import Mesh
from jax.sharding import PartitionSpec as P

D = 512
H = 8
DH = 64
SLOT = 256
HIST = 16
EPS = 1e-05
META = 16
ROWS = 5 * DH
PIECE = ROWS // 4
F32 = jnp.float32
BF16 = jnp.bfloat16
DP = ("y", "x", "zlo")
COL = ("zhi", "core")
VMEM = pl.BlockSpec(memory_space=pltpu.VMEM)
SMEM = pl.BlockSpec(memory_space=pltpu.SMEM)


def params(mib):
    return pltpu.CompilerParams(vmem_limit_bytes=mib * 1024 * 1024)


def spread_kernel(route, lengths, rows, sent):
    sent[...] = jnp.zeros_like(sent)
    for h in range(HIST):
        group = route[h, 0]
        sent[group, :DH, :] = rows[h]
        slot = (route[h, 1] + 1).astype(F32)
        count = lengths[h].astype(F32)
        sent[group, DH:, : SLOT // 2] = jnp.full((META, SLOT // 2), slot, F32).astype(BF16)
        sent[group, DH:, SLOT // 2 :] = jnp.full((META, SLOT // 2), count, F32).astype(BF16)


def settle_kernel(arrived, rows, meta):
    groups = arrived.shape[0]
    for group in range(groups):
        note = arrived[group, DH:, :].astype(F32)
        slot = jnp.max(note[:, : SLOT // 2]).astype(jnp.int32)
        count = jnp.max(note[:, SLOT // 2 :]).astype(jnp.int32)

        @pl.when(slot > 0)
        def _():
            rows[slot - 1] = arrived[group, :DH, :]
            meta[0, slot - 1] = group
            meta[1, slot - 1] = count


def return_kernel(meta, rows, sent):
    sent[...] = jnp.zeros_like(sent)
    for k in range(HIST):
        sent[meta[0, k]] = rows[k]


def collect_kernel(route, arrived, rows):
    for h in range(HIST):
        rows[h] = arrived[route[h, 0]]


def tn(a, b):
    return lax.dot_general(a, b, (((0,), (0,)), ((), ())), preferred_element_type=F32)


def nt(a, b):
    return lax.dot_general(a, b, (((1,), (1,)), ((), ())), preferred_element_type=F32)


def nn(a, b):
    return lax.dot_general(a, b, (((1,), (0,)), ((), ())), preferred_element_type=F32)


def silu_parts(z):
    sigma = 0.5 * jnp.tanh(0.5 * z) + 0.5
    silu = z * sigma
    return silu, sigma + silu * (1.0 - sigma)


def layer_kernel(
    place,
    meta,
    xa,
    gy_ref,
    wg,
    mixed,
    gfeat,
    mine,
    other,
    x_s,
    norm_s,
    xn_s,
    slope_s,
    proj_s,
    att_s,
    w_s,
    sl_s,
    gated_s,
    gy_s,
    gatt_s,
    gpre_s,
    sum_s,
    wo_s,
    gwo_s,
):
    tokens = 2 * SLOT
    col = place[0]
    core = place[1]
    factor = BF16(DH**-0.5)
    for i in range(2):
        lanes = slice(i * SLOT, (i + 1) * SLOT)
        x_s[:, lanes] = xa[:, i].reshape(D, SLOT).astype(F32)
        gy_s[:, lanes] = gy_ref[i]
    wo_s[...] = wg[:, 4 * DH :, :].reshape(D, D)

    inv_in = []
    for i in range(tokens // 128):
        lanes = slice(i * 128, (i + 1) * 128)
        x = x_s[:, lanes]
        centred = x - jnp.mean(x, axis=0, keepdims=True)
        inv = lax.rsqrt(jnp.mean(centred * centred, axis=0, keepdims=True) + EPS)
        normed = centred * inv
        inv_in.append(inv)
        norm_s[:, lanes] = normed
        xn_s[:, lanes] = normed.astype(BF16)

    key_at = lax.broadcasted_iota(jnp.int32, (SLOT, SLOT), 0)
    query_at = lax.broadcasted_iota(jnp.int32, (SLOT, SLOT), 1)

    def forward_head(h, sums):
        silu, slope = silu_parts(nn(wg[h, : 4 * DH, :], xn_s[...]))
        slope_s[h] = slope
        proj_s[h] = silu.astype(BF16)
        parts = []
        for i in range(2):
            lanes = slice(i * SLOT, (i + 1) * SLOT)
            value = proj_s[h, DH : 2 * DH, lanes]
            query = proj_s[h, 2 * DH : 3 * DH, lanes]
            key = proj_s[h, 3 * DH :, lanes] * factor
            live = (key_at <= query_at) & (query_at < meta[1, 2 * col + i])
            silu_w, slope_w = silu_parts(tn(key, query))
            weights = jnp.where(live, silu_w, 0.0).astype(BF16)
            w_s[h, i] = weights
            sl_s[h, i] = jnp.where(live, slope_w, 0.0).astype(BF16)
            parts.append(nn(value, weights))
        att = jnp.concatenate(parts, axis=1)
        att_s[pl.ds(h * DH, DH), :] = att
        return (
            sums[0] + jnp.sum(att, axis=0, keepdims=True),
            sums[1] + jnp.sum(att * att, axis=0, keepdims=True),
        )

    zero = jnp.zeros((1, tokens), F32)
    totals, squares = lax.fori_loop(0, H, forward_head, (zero, zero))
    mean = totals / D
    inv_out = lax.rsqrt(squares / D - mean * mean + EPS)

    def gate_head(h, carry):
        rows = pl.ds(h * DH, DH)
        normed = (att_s[rows, :] - mean) * inv_out
        att_s[rows, :] = normed
        gated_s[rows, :] = (normed * proj_s[h, :DH, :].astype(F32)).astype(BF16)
        return carry

    lax.fori_loop(0, H, gate_head, 0)
    out = (x_s[...] + tn(wo_s[...], gated_s[...])).astype(BF16)
    for i in range(2):
        mixed[:, i] = out[:, i * SLOT : (i + 1) * SLOT].reshape(H, DH, SLOT)

    x_s[...] = nn(wo_s[...], gy_s[...])
    gwo_s[...] = nt(gated_s[...], gy_s[...]).astype(BF16)

    def sum_head(h, sums):
        rows = pl.ds(h * DH, DH)
        grad = x_s[rows, :] * proj_s[h, :DH, :].astype(F32)
        return (
            sums[0] + jnp.sum(grad, axis=0, keepdims=True),
            sums[1] + jnp.sum(grad * att_s[rows, :], axis=0, keepdims=True),
        )

    first, second = lax.fori_loop(0, H, sum_head, (zero, zero))
    first = first / D
    second = second / D

    def store_grad(ref, at, grad_win, grad_wout):
        last = 4 * DH - 3 * PIECE
        for part in range(4):
            lanes = slice(part * 128, (part + 1) * 128)
            for cut in range(3):
                ref[4 * part + cut, at] = grad_win[cut * PIECE : (cut + 1) * PIECE, lanes]
            ref[4 * part + 3, at, :last, :] = grad_win[3 * PIECE :, lanes]
            ref[4 * part + 3, at, last:, :] = grad_wout[:, lanes]

    sum_s[...] = jnp.zeros_like(sum_s)

    def backward_head(h, carry):
        rows = pl.ds(h * DH, DH)
        grad_gated = x_s[rows, :]
        normed = att_s[rows, :]
        grad_normo = grad_gated * proj_s[h, :DH, :].astype(F32)
        gatt_s[...] = (inv_out * (grad_normo - first - normed * second)).astype(BF16)
        gpre_s[:DH, :] = (grad_gated * normed * slope_s[h, :DH, :]).astype(BF16)
        for i in range(2):
            lanes = slice(i * SLOT, (i + 1) * SLOT)
            value = proj_s[h, DH : 2 * DH, lanes]
            query = proj_s[h, 2 * DH : 3 * DH, lanes] * factor
            key = proj_s[h, 3 * DH :, lanes] * factor
            grad = gatt_s[:, lanes]
            grad_scores = (tn(value, grad) * sl_s[h, i].astype(F32)).astype(BF16)
            grad_value = nt(grad, w_s[h, i])
            grad_query = nn(key, grad_scores)
            grad_key = nt(query, grad_scores)
            for c, part in ((1, grad_value), (2, grad_query), (3, grad_key)):
                at = slice(c * DH, (c + 1) * DH)
                gpre_s[at, lanes] = (part * slope_s[h, at, lanes]).astype(BF16)
        grad_win = nt(gpre_s[...], xn_s[...]).astype(BF16)
        grad_wout = gwo_s[rows, :]

        @pl.when(h % 2 == core)
        def _():
            store_grad(mine, h // 2, grad_win, grad_wout)

        @pl.when(h % 2 != core)
        def _():
            store_grad(other, h // 2, grad_win, grad_wout)

        sum_s[...] += tn(wg[h, : 4 * DH, :], gpre_s[...])
        return carry

    lax.fori_loop(0, H, backward_head, 0)
    for i in range(tokens // 128):
        lanes = slice(i * 128, (i + 1) * 128)
        grad = sum_s[:, lanes]
        normed = norm_s[:, lanes]
        lead = jnp.mean(grad, axis=0, keepdims=True)
        cross = jnp.mean(grad * normed, axis=0, keepdims=True)
        total = gy_s[:, lanes].astype(F32) + inv_in[i] * (grad - lead - normed * cross)
        here = slice(i % 2 * 128, (i % 2 + 1) * 128)
        gfeat[:, i // 2, :, here] = total.astype(BF16).reshape(H, DH, 128)


def run_layer(place, meta, xa, grad_y, wg):
    tokens = 2 * SLOT
    piece = jax.ShapeDtypeStruct((16, 4, PIECE, 128), BF16)
    block = jax.ShapeDtypeStruct((H, 2, DH, SLOT), BF16)
    return pl.pallas_call(
        layer_kernel,
        out_shape=(block, block, piece, piece),
        in_specs=[SMEM, SMEM, VMEM, VMEM, VMEM],
        out_specs=(VMEM, VMEM, VMEM, VMEM),
        scratch_shapes=[
            pltpu.VMEM((D, tokens), F32),
            pltpu.VMEM((D, tokens), F32),
            pltpu.VMEM((D, tokens), BF16),
            pltpu.VMEM((H, 4 * DH, tokens), F32),
            pltpu.VMEM((H, 4 * DH, tokens), BF16),
            pltpu.VMEM((D, tokens), F32),
            pltpu.VMEM((H, 2, SLOT, SLOT), BF16),
            pltpu.VMEM((H, 2, SLOT, SLOT), BF16),
            pltpu.VMEM((D, tokens), BF16),
            pltpu.VMEM((D, tokens), BF16),
            pltpu.VMEM((DH, tokens), BF16),
            pltpu.VMEM((4 * DH, tokens), BF16),
            pltpu.VMEM((D, tokens), F32),
            pltpu.VMEM((D, D), BF16),
            pltpu.VMEM((D, D), BF16),
        ],
        compiler_params=params(48),
    )(place, meta, xa, grad_y, wg)


def swap(x, axes):
    return lax.all_to_all(x, axes, split_axis=0, concat_axis=0, tiled=True)


def on_device(features, cotangent, lengths, route, w_in, w_out):
    groups = lax.axis_size(DP)
    col = lax.axis_index(COL)
    place = jnp.stack([col, lax.axis_index("core")]).astype(jnp.int32)

    packed = jnp.concatenate([w_in.transpose(0, 2, 1).reshape(4 * DH, D), w_out], axis=0)
    wg = lax.all_gather(packed, COL)
    sent = pl.pallas_call(
        spread_kernel,
        out_shape=jax.ShapeDtypeStruct((groups, DH + META, SLOT), BF16),
        in_specs=[SMEM, SMEM, VMEM],
        out_specs=VMEM,
        compiler_params=params(16),
    )(route, lengths, features)
    rows, meta = pl.pallas_call(
        settle_kernel,
        out_shape=(
            jax.ShapeDtypeStruct((HIST, DH, SLOT), BF16),
            jax.ShapeDtypeStruct((2, HIST), jnp.int32),
        ),
        in_specs=[VMEM],
        out_specs=(VMEM, SMEM),
        compiler_params=params(16),
    )(swap(sent, DP))
    xa = swap(rows, COL).reshape(H, 2, DH, SLOT)
    grad_y = lax.dynamic_slice_in_dim(cotangent, 2 * col, 2, 0)
    mixed, gfeat, mine, other = run_layer(place, meta, xa, grad_y, wg)

    came = lax.ppermute(other, "core", [(0, 1), (1, 0)])
    half = (mine.astype(F32) + came.astype(F32)).astype(BF16)
    part = jnp.sum(swap(half, ("y", "x")).reshape(16, 4, PIECE, 128).astype(F32), axis=0)
    part = part.astype(BF16).reshape(8, PIECE // 2, 128)
    part = jnp.sum(swap(part, ("zhi", "zlo")).astype(F32), axis=0).astype(BF16)
    whole = swap(jnp.broadcast_to(part[None], (groups, PIECE // 2, 128)), DP)
    whole = whole.reshape(4, 4, 2, PIECE // 2, 128).transpose(1, 2, 3, 0, 4).reshape(ROWS, D)
    whole = whole.astype(F32) * (float(HIST * groups * SLOT) ** -0.5)
    grad_in = whole[: 4 * DH].reshape(4, DH, D).transpose(0, 2, 1)
    grad_out = whole[4 * DH :]

    home = swap(gfeat.reshape(HIST, DH, SLOT), COL)
    back = pl.pallas_call(
        return_kernel,
        out_shape=jax.ShapeDtypeStruct((groups, DH, SLOT), BF16),
        in_specs=[SMEM, VMEM],
        out_specs=VMEM,
        compiler_params=params(16),
    )(meta, home)
    grad_features = pl.pallas_call(
        collect_kernel,
        out_shape=jax.ShapeDtypeStruct((HIST, DH, SLOT), BF16),
        in_specs=[SMEM, VMEM],
        out_specs=VMEM,
        compiler_params=params(16),
    )(route, swap(back, DP))
    return (swap(mixed.reshape(HIST, DH, SLOT), COL), grad_features, grad_in, grad_out)


def solution(mesh):
    split = Mesh(mesh.devices.reshape(4, 4, 2, 4, 2), ("y", "x", "zlo", "zhi", "core"))
    in_specs = (P(DP, COL, None), P(DP, None, None), P(DP), P(DP, None), P(None, None, COL), P(COL, None))
    out_specs = (P(DP, COL, None), P(DP, COL, None), P(None, None, COL), P(COL, None))
    return jax.shard_map(
        on_device, mesh=split, in_specs=in_specs, out_specs=out_specs, check_vma=False
    )
```

```python
import jax
import jax.numpy as jnp
from jax import lax
from jax.experimental import pallas as pl
from jax.experimental.pallas import tpu as pltpu
from jax.sharding import Mesh
from jax.sharding import PartitionSpec as P

D = 512
H = 8
DH = 64
SLOT = 256
HIST = 16
EPS = 1e-05
META = 16
ROWS = 5 * DH
PIECE = ROWS // 4
F32 = jnp.float32
BF16 = jnp.bfloat16
DP = ("y", "x", "zlo")
COL = ("zhi", "core")
VMEM = pl.BlockSpec(memory_space=pltpu.VMEM)
SMEM = pl.BlockSpec(memory_space=pltpu.SMEM)


def params(mib):
    return pltpu.CompilerParams(vmem_limit_bytes=mib * 1024 * 1024)


def spread_kernel(route, lengths, rows, sent):
    sent[...] = jnp.zeros_like(sent)
    for h in range(HIST):
        group = route[h, 0]
        sent[group, :DH, :] = rows[h]
        slot = (route[h, 1] + 1).astype(F32)
        count = lengths[h].astype(F32)
        sent[group, DH:, : SLOT // 2] = jnp.full((META, SLOT // 2), slot, F32).astype(BF16)
        sent[group, DH:, SLOT // 2 :] = jnp.full((META, SLOT // 2), count, F32).astype(BF16)


def settle_kernel(arrived, rows, meta):
    codes = []
    for group in range(arrived.shape[0]):
        note = arrived[group, DH:, :].astype(F32)[:8]
        code = jnp.max(note[:, : SLOT // 2] * 512.0 + note[:, SLOT // 2 :])
        codes.append(code.astype(jnp.int32))
    for group, code in enumerate(codes):

        @pl.when(code >= 512)
        def _():
            slot = lax.shift_right_logical(code, 9) - 1
            rows[slot] = arrived[group, :DH, :]
            meta[0, slot] = group
            meta[1, slot] = code & 511


def return_kernel(meta, rows, sent):
    sent[...] = jnp.zeros_like(sent)
    for k in range(HIST):
        sent[meta[0, k]] = rows[k]


def collect_kernel(route, arrived, rows):
    for h in range(HIST):
        rows[h] = arrived[route[h, 0]]


def tn(a, b):
    return lax.dot_general(a, b, (((0,), (0,)), ((), ())), preferred_element_type=F32)


def nt(a, b):
    return lax.dot_general(a, b, (((1,), (1,)), ((), ())), preferred_element_type=F32)


def nn(a, b):
    return lax.dot_general(a, b, (((1,), (0,)), ((), ())), preferred_element_type=F32)


def silu_parts(z):
    sigma = 0.5 * jnp.tanh(0.5 * z) + 0.5
    silu = z * sigma
    return silu, sigma + silu * (1.0 - sigma)


def wrap(position, back):
    return lax.rem(position - back + 4, 4)


def forward_kernel(
    place,
    meta,
    xa,
    own0,
    own1,
    own2,
    own3,
    far0,
    far1,
    far2,
    far3,
    mixed,
    win,
    wout,
    xn,
    inv_in,
    slopes,
    proj,
    weights,
    score_slopes,
    out_norm,
    inv_out,
    gated,
    x_s,
):
    tokens = 2 * SLOT
    col = place[0]
    core = place[1]
    factor = BF16(DH**-0.5)
    for i in range(2):
        x_s[:, i * SLOT : (i + 1) * SLOT] = xa[:, i].reshape(D, SLOT).astype(F32)
    for side, refs, along in ((core, (own0, own1, own2, own3), place[3]), (1 - core, (far0, far1, far2, far3), place[4])):
        for k in range(4):
            piece = wrap(along, k)
            for z in range(4):
                head = 2 * wrap(place[2], z) + side
                at = pl.multiple_of(piece * DH, DH)
                win[head, pl.ds(at, DH), :] = refs[k][z, :DH, :]
                at = pl.multiple_of(head * DH + piece * (DH // 4), DH // 4)
                wout[pl.ds(at, DH // 4), :] = refs[k][z, DH:, :]

    for i in range(tokens // 128):
        lanes = slice(i * 128, (i + 1) * 128)
        x = x_s[:, lanes]
        centred = x - jnp.mean(x, axis=0, keepdims=True)
        inv = lax.rsqrt(jnp.mean(centred * centred, axis=0, keepdims=True) + EPS)
        inv_in[:, lanes] = inv
        xn[:, lanes] = (centred * inv).astype(BF16)

    key_at = lax.broadcasted_iota(jnp.int32, (SLOT, SLOT), 0)
    query_at = lax.broadcasted_iota(jnp.int32, (SLOT, SLOT), 1)

    def head_step(h, sums):
        silu, slope = silu_parts(nn(win[h], xn[...]))
        slopes[h] = slope.astype(BF16)
        proj[h] = silu.astype(BF16)
        parts = []
        for i in range(2):
            lanes = slice(i * SLOT, (i + 1) * SLOT)
            value = proj[h, DH : 2 * DH, lanes]
            query = proj[h, 2 * DH : 3 * DH, lanes]
            key = proj[h, 3 * DH :, lanes] * factor
            live = (key_at <= query_at) & (query_at < meta[1, 2 * col + i])
            silu_w, slope_w = silu_parts(tn(key, query))
            weight = jnp.where(live, silu_w, 0.0).astype(BF16)
            weights[h, i] = weight
            score_slopes[h, i] = jnp.where(live, slope_w, 0.0).astype(BF16)
            parts.append(nn(value, weight))
        att = jnp.concatenate(parts, axis=1)
        out_norm[pl.ds(h * DH, DH), :] = att
        return (
            sums[0] + jnp.sum(att, axis=0, keepdims=True),
            sums[1] + jnp.sum(att * att, axis=0, keepdims=True),
        )

    zero = jnp.zeros((1, tokens), F32)
    totals, squares = lax.fori_loop(0, H, head_step, (zero, zero))
    mean = totals / D
    inv = lax.rsqrt(squares / D - mean * mean + EPS)
    inv_out[...] = inv

    def gate_step(h, carry):
        rows = pl.ds(h * DH, DH)
        normed = (out_norm[rows, :] - mean) * inv
        out_norm[rows, :] = normed
        gated[rows, :] = (normed * proj[h, :DH, :].astype(F32)).astype(BF16)
        return carry

    lax.fori_loop(0, H, gate_step, 0)
    out = (x_s[...] + tn(wout[...], gated[...])).astype(BF16)
    for i in range(2):
        mixed[:, i] = out[:, i * SLOT : (i + 1) * SLOT].reshape(H, DH, SLOT)


def backward_kernel(
    place,
    gy_ref,
    win,
    wout,
    xn,
    inv_in,
    slopes,
    proj,
    weights,
    score_slopes,
    out_norm,
    inv_out,
    gated,
    gfeat,
    mine,
    other,
    grad_s,
    gy_s,
    gatt_s,
    gpre_s,
    sum_s,
    gwo_s,
):
    tokens = 2 * SLOT
    core = place[1]
    factor = BF16(DH**-0.5)
    for i in range(2):
        gy_s[:, i * SLOT : (i + 1) * SLOT] = gy_ref[i]
    grad_s[...] = nn(wout[...], gy_s[...])
    gwo_s[...] = nt(gated[...], gy_s[...]).astype(BF16)

    def sum_step(h, sums):
        rows = pl.ds(h * DH, DH)
        grad = grad_s[rows, :] * proj[h, :DH, :].astype(F32)
        return (
            sums[0] + jnp.sum(grad, axis=0, keepdims=True),
            sums[1] + jnp.sum(grad * out_norm[rows, :], axis=0, keepdims=True),
        )

    zero = jnp.zeros((1, tokens), F32)
    first, second = lax.fori_loop(0, H, sum_step, (zero, zero))
    first = first / D
    second = second / D
    inv = inv_out[...]

    def store_grad(ref, at, grad_win, grad_wout):
        for part in range(4):
            lanes = slice(part * 128, (part + 1) * 128)
            for c in range(4):
                ref[4 * part + c, at, :DH, :] = grad_win[c * DH : (c + 1) * DH, lanes]
                ref[4 * part + c, at, DH:, :] = grad_wout[c * DH // 4 : (c + 1) * DH // 4, lanes]

    sum_s[...] = jnp.zeros_like(sum_s)

    def head_step(h, carry):
        rows = pl.ds(h * DH, DH)
        grad_gated = grad_s[rows, :]
        normed = out_norm[rows, :]
        grad_normo = grad_gated * proj[h, :DH, :].astype(F32)
        gatt_s[...] = (inv * (grad_normo - first - normed * second)).astype(BF16)
        gpre_s[:DH, :] = (grad_gated * normed * slopes[h, :DH, :].astype(F32)).astype(BF16)
        for i in range(2):
            lanes = slice(i * SLOT, (i + 1) * SLOT)
            value = proj[h, DH : 2 * DH, lanes]
            query = proj[h, 2 * DH : 3 * DH, lanes] * factor
            key = proj[h, 3 * DH :, lanes] * factor
            grad = gatt_s[:, lanes]
            grad_scores = (tn(value, grad) * score_slopes[h, i].astype(F32)).astype(BF16)
            grad_value = nt(grad, weights[h, i])
            grad_query = nn(key, grad_scores)
            grad_key = nt(query, grad_scores)
            for c, part in ((1, grad_value), (2, grad_query), (3, grad_key)):
                at = slice(c * DH, (c + 1) * DH)
                gpre_s[at, lanes] = (part * slopes[h, at, lanes].astype(F32)).astype(BF16)
        grad_win = nt(gpre_s[...], xn[...]).astype(BF16)
        grad_wout = gwo_s[rows, :]

        @pl.when(h % 2 == core)
        def _():
            store_grad(mine, h // 2, grad_win, grad_wout)

        @pl.when(h % 2 != core)
        def _():
            store_grad(other, h // 2, grad_win, grad_wout)

        sum_s[...] += tn(win[h], gpre_s[...])
        return carry

    lax.fori_loop(0, H, head_step, 0)
    for i in range(tokens // 128):
        lanes = slice(i * 128, (i + 1) * 128)
        grad = sum_s[:, lanes]
        normed = xn[:, lanes].astype(F32)
        lead = jnp.mean(grad, axis=0, keepdims=True)
        cross = jnp.mean(grad * normed, axis=0, keepdims=True)
        total = gy_s[:, lanes].astype(F32) + inv_in[:, lanes] * (grad - lead - normed * cross)
        here = slice(i % 2 * 128, (i % 2 + 1) * 128)
        gfeat[:, i // 2, :, here] = total.astype(BF16).reshape(H, DH, 128)


def run_forward(place, meta, xa, pieces):
    tokens = 2 * SLOT
    shape = jax.ShapeDtypeStruct
    return pl.pallas_call(
        forward_kernel,
        out_shape=(
            shape((H, 2, DH, SLOT), BF16),
            shape((H, 4 * DH, D), BF16),
            shape((D, D), BF16),
            shape((D, tokens), BF16),
            shape((1, tokens), F32),
            shape((H, 4 * DH, tokens), BF16),
            shape((H, 4 * DH, tokens), BF16),
            shape((H, 2, SLOT, SLOT), BF16),
            shape((H, 2, SLOT, SLOT), BF16),
            shape((D, tokens), F32),
            shape((1, tokens), F32),
            shape((D, tokens), BF16),
        ),
        in_specs=[SMEM, SMEM] + [VMEM] * 9,
        out_specs=(VMEM,) * 12,
        scratch_shapes=[pltpu.VMEM((D, tokens), F32)],
        compiler_params=params(28),
    )(place, meta, xa, *pieces)


def run_backward(place, grad_y, saved):
    tokens = 2 * SLOT
    piece = jax.ShapeDtypeStruct((16, 4, PIECE, 128), BF16)
    return pl.pallas_call(
        backward_kernel,
        out_shape=(jax.ShapeDtypeStruct((H, 2, DH, SLOT), BF16), piece, piece),
        in_specs=[SMEM] + [VMEM] * 12,
        out_specs=(VMEM,) * 3,
        scratch_shapes=[
            pltpu.VMEM((D, tokens), F32),
            pltpu.VMEM((D, tokens), BF16),
            pltpu.VMEM((DH, tokens), BF16),
            pltpu.VMEM((4 * DH, tokens), BF16),
            pltpu.VMEM((D, tokens), F32),
            pltpu.VMEM((D, D), BF16),
        ],
        compiler_params=params(32),
    )(place, grad_y, *saved)


def finish_kernel(arrived, grad_in, grad_out):
    factor = float(HIST * 32 * SLOT) ** -0.5
    for part in range(4):
        lanes = slice(part * 128, (part + 1) * 128)
        for c in range(4):
            block = arrived[4 * part + c].astype(F32) * factor
            grad_in[c, :, lanes] = block[:DH]
            grad_out[c * DH // 4 : (c + 1) * DH // 4, lanes] = block[DH:]


def gather_weights(w_in, w_out, place):
    along = place[3]
    proj = lax.dynamic_index_in_dim(w_in.transpose(0, 2, 1), along, 0, keepdims=False)
    rows = lax.dynamic_slice_in_dim(w_out, along * (DH // 4), DH // 4, 0)
    piece = jnp.concatenate([proj, rows], axis=0)
    shards = [piece]
    for k in range(1, 4):
        shards.append(lax.ppermute(piece, "zhi", [(i, (i + k) % 4) for i in range(4)]))
    own = [jnp.stack(shards)]
    for k in range(1, 4):
        pairs = []
        for y in range(4):
            for x in range(4):
                pairs.append(((4 * y + x) * 2, (4 * y + (x + k) % 4) * 2))
                pairs.append(((4 * y + x) * 2 + 1, (4 * ((y + k) % 4) + x) * 2 + 1))
        own.append(lax.ppermute(own[0], ("y", "x", "core"), pairs))
    return own + [lax.ppermute(part, "core", [(0, 1), (1, 0)]) for part in own]


def swap(x, axes):
    return lax.all_to_all(x, axes, split_axis=0, concat_axis=0, tiled=True)


def on_device(features, cotangent, lengths, route, w_in, w_out):
    groups = lax.axis_size(DP)
    col = lax.axis_index(COL)
    core = lax.axis_index("core")
    zhi = lax.axis_index("zhi")
    x = lax.axis_index("x")
    y = lax.axis_index("y")
    along = jnp.where(core == 0, x, y)
    place = jnp.stack([col, core, zhi, along, x + y - along]).astype(jnp.int32)

    sent = pl.pallas_call(
        spread_kernel,
        out_shape=jax.ShapeDtypeStruct((groups, DH + META, SLOT), BF16),
        in_specs=[SMEM, SMEM, VMEM],
        out_specs=VMEM,
        compiler_params=params(16),
    )(route, lengths, features)
    arrived = swap(sent, DP)
    pieces = gather_weights(w_in, w_out, place)
    rows, meta = pl.pallas_call(
        settle_kernel,
        out_shape=(
            jax.ShapeDtypeStruct((HIST, DH, SLOT), BF16),
            jax.ShapeDtypeStruct((2, HIST), jnp.int32),
        ),
        in_specs=[VMEM],
        out_specs=(VMEM, SMEM),
        compiler_params=params(16),
    )(arrived)
    xa = swap(rows, COL).reshape(H, 2, DH, SLOT)
    grad_y = lax.dynamic_slice_in_dim(cotangent, 2 * col, 2, 0)
    mixed, *saved = run_forward(place, meta, xa, pieces)
    mixed = swap(mixed.reshape(HIST, DH, SLOT), COL)
    gfeat, mine, other = run_backward(place, grad_y, saved)

    came = lax.ppermute(other, "core", [(0, 1), (1, 0)])
    home = swap(gfeat.reshape(HIST, DH, SLOT), COL)
    half = (mine.astype(F32) + came.astype(F32)).astype(BF16)
    part = jnp.sum(swap(half, ("y", "x")).reshape(16, 4, PIECE, 128).astype(F32), axis=0)
    part = part.astype(BF16)
    total = lax.dynamic_index_in_dim(part, zhi, 0, keepdims=False).astype(F32)
    for k in range(1, 4):
        chunk = lax.dynamic_index_in_dim(part, (zhi + k) % 4, 0, keepdims=False)
        total = total + lax.ppermute(chunk, "zhi", [(i, (i + k) % 4) for i in range(4)]).astype(F32)
    pair = lax.ppermute(total.astype(BF16), "zlo", [(0, 1), (1, 0)])
    part = (total + pair.astype(F32)).astype(BF16)
    whole = swap(jnp.broadcast_to(part[None], (16, PIECE, 128)), ("y", "x"))
    grad_in, grad_out = pl.pallas_call(
        finish_kernel,
        out_shape=(jax.ShapeDtypeStruct((4, DH, D), F32), jax.ShapeDtypeStruct((DH, D), F32)),
        in_specs=[VMEM],
        out_specs=(VMEM, VMEM),
        compiler_params=params(16),
    )(whole)

    back = pl.pallas_call(
        return_kernel,
        out_shape=jax.ShapeDtypeStruct((groups, DH, SLOT), BF16),
        in_specs=[SMEM, VMEM],
        out_specs=VMEM,
        compiler_params=params(16),
    )(meta, home)
    grad_features = pl.pallas_call(
        collect_kernel,
        out_shape=jax.ShapeDtypeStruct((HIST, DH, SLOT), BF16),
        in_specs=[SMEM, VMEM],
        out_specs=VMEM,
        compiler_params=params(16),
    )(route, swap(back, DP))
    return (mixed, grad_features, grad_in.transpose(0, 2, 1), grad_out)


def solution(mesh):
    split = Mesh(mesh.devices.reshape(4, 4, 2, 4, 2), ("y", "x", "zlo", "zhi", "core"))
    in_specs = (P(DP, COL, None), P(DP, None, None), P(DP), P(DP, None), P(None, None, COL), P(COL, None))
    out_specs = (P(DP, COL, None), P(DP, COL, None), P(None, None, COL), P(COL, None))
    return jax.shard_map(
        on_device, mesh=split, in_specs=in_specs, out_specs=out_specs, check_vma=False
    )
```

```python
import jax
import jax.numpy as jnp
from jax import lax
from jax.experimental import pallas as pl
from jax.experimental.pallas import tpu as pltpu
from jax.sharding import Mesh
from jax.sharding import PartitionSpec as P

D = 512
H = 8
DH = 64
SLOT = 256
HIST = 16
EPS = 1e-05
META = 16
TILE = 128
ROWS = 5 * DH
PIECE = ROWS // 4
F32 = jnp.float32
BF16 = jnp.bfloat16
DP = ("y", "x", "zlo")
COL = ("zhi", "core")
VMEM = pl.BlockSpec(memory_space=pltpu.VMEM)
SMEM = pl.BlockSpec(memory_space=pltpu.SMEM)
ANY = pl.BlockSpec(memory_space=pl.ANY)


def params(mib):
    return pltpu.CompilerParams(vmem_limit_bytes=mib * 1024 * 1024)


def cost(flops, moved):
    return pl.CostEstimate(flops=flops, bytes_accessed=moved, transcendentals=0)


def spread_kernel(place, route, lengths, rows, proj, wout, sent, piece):
    along = place[3]
    piece[:DH, :] = proj[along]
    piece[DH:, :] = wout[pl.ds(pl.multiple_of(along * (DH // 4), DH // 4), DH // 4), :]
    sent[...] = jnp.zeros_like(sent)
    for h in range(HIST):
        group = route[0, h]
        sent[group, :DH, :] = rows[h]
        slot = (route[1, h] + 1).astype(F32)
        count = lengths[h].astype(F32)
        sent[group, DH:, : SLOT // 2] = jnp.full((META, SLOT // 2), slot, F32).astype(BF16)
        sent[group, DH:, SLOT // 2 :] = jnp.full((META, SLOT // 2), count, F32).astype(BF16)


def settle_kernel(arrived, shard1, shard2, shard3, rows, meta):
    codes = []
    for group in range(arrived.shape[0]):
        note = arrived[group, DH:, :].astype(F32)[:8]
        code = jnp.max(note[:, : SLOT // 2] * 512.0 + note[:, SLOT // 2 :])
        codes.append(code.astype(jnp.int32))
    for group, code in enumerate(codes):

        @pl.when(code >= 512)
        def _():
            slot = lax.shift_right_logical(code, 9) - 1
            rows[slot] = arrived[group, :DH, :]
            meta[0, slot] = group
            meta[1, slot] = code & 511


def add_kernel(place, mine, came, sum0, sum1, sum2, sum3):
    core = place[1]
    for k, total in enumerate((sum0, sum1, sum2, sum3)):
        ahead = lax.rem(place[3] + k, 4)
        for j in range(4):
            piece = jnp.where(core == 0, 4 * j + ahead, 4 * ahead + j)
            total[j] = (mine[piece].astype(F32) + came[piece].astype(F32)).astype(BF16)


def cross_kernel(place, kept, came1, came2, came3, sum0, sum1, sum2, sum3):
    for k, total in enumerate((sum0, sum1, sum2, sum3)):
        j = lax.rem(place[4] + k, 4)
        part = kept[j].astype(F32)
        for came in (came1, came2, came3):
            part = part + came[j].astype(F32)
        total[...] = part.astype(BF16)


def depth_kernel(place, kept, came1, came2, came3, sum0, sum1, sum2, sum3):
    for k, total in enumerate((sum0, sum1, sum2, sum3)):
        z = lax.rem(place[2] + k, 4)
        part = kept[z].astype(F32)
        for came in (came1, came2, came3):
            part = part + came[z].astype(F32)
        total[...] = part.astype(BF16) if k else part


def last_kernel(kept, came1, came2, came3, total, rounded):
    part = kept[...]
    for came in (came1, came2, came3):
        part = part + came[...].astype(F32)
    total[...] = part
    rounded[...] = part.astype(BF16)


def repeat_kernel(total, came, after, whole):
    summed = (total[...] + came[...].astype(F32)).astype(BF16)
    for group in range(whole.shape[0]):
        whole[group] = summed


def pair_kernel(same, came, after, pair0, pair1, pair2, pair3):
    for k, pair in enumerate((pair0, pair1, pair2, pair3)):
        pair[0] = same[k]
        pair[1] = came[k]


def return_kernel(meta, rows, after, sent):
    sent[...] = jnp.zeros_like(sent)
    for k in range(HIST):
        sent[meta[0, k]] = rows[k]


def collect_kernel(place, route, arrived, pair0, pair1, pair2, pair3, rows, mixed):
    for h in range(HIST):
        rows[h] = arrived[route[0, h]]
    core = place[1]
    for k, pair in enumerate((pair0, pair1, pair2, pair3)):
        for side in range(2):
            owner = 2 * wrap(place[2], k) + (core if side == 0 else 1 - core)
            for i in range(2):
                mixed[2 * owner + i] = pair[side, i]


def tn(a, b):
    return lax.dot_general(a, b, (((0,), (0,)), ((), ())), preferred_element_type=F32)


def nt(a, b):
    return lax.dot_general(a, b, (((1,), (1,)), ((), ())), preferred_element_type=F32)


def nn(a, b):
    return lax.dot_general(a, b, (((1,), (0,)), ((), ())), preferred_element_type=F32)


def silu_parts(half):
    t = jnp.tanh(half)
    up = 1.0 + t
    silu = half * up
    return silu, up + silu * (1.0 - t)


def live_row(meta, col):
    at = lax.broadcasted_iota(jnp.int32, (1, SLOT), 1)
    rows = [(at < meta[1, 2 * col + i]).astype(F32) for i in range(2)]
    return jnp.concatenate(rows, axis=1)


def wrap(position, back):
    return lax.rem(position - back + 4, 4)


def split_chunks(place, chunks, same, cross):
    for k in range(4):
        goal = 2 * lax.rem(place[2] + k, 4)
        same[k] = chunks[goal + place[1]]
        cross[k] = chunks[goal + 1 - place[1]]


def forward_kernel(
    place,
    meta,
    xa,
    own0,
    own1,
    own2,
    own3,
    far0,
    far1,
    far2,
    far3,
    msame,
    mcross,
    win,
    wout,
    xn,
    inv_in,
    slopes,
    proj,
    weights,
    score_slopes,
    out_norm,
    inv_out,
    gated,
    mixed,
    x_s,
):
    tokens = 2 * SLOT
    col = place[0]
    core = place[1]
    for i in range(2):
        x_s[:, i * SLOT : (i + 1) * SLOT] = xa[:, i].reshape(D, SLOT).astype(F32)
    for side, refs, along in ((core, (own0, own1, own2, own3), place[3]), (1 - core, (far0, far1, far2, far3), place[4])):
        for k in range(4):
            piece = wrap(along, k)
            for z in range(4):
                head = 2 * wrap(place[2], z) + side
                at = pl.multiple_of(piece * DH, DH)
                win[head, pl.ds(at, DH), :] = refs[k][z, :DH, :]
                at = pl.multiple_of(head * DH + piece * (DH // 4), DH // 4)
                wout[pl.ds(at, DH // 4), :] = refs[k][z, DH:, :]

    for i in range(tokens // 128):
        lanes = slice(i * 128, (i + 1) * 128)
        x = x_s[:, lanes]
        centred = x - jnp.mean(x, axis=0, keepdims=True)
        inv = lax.rsqrt(jnp.mean(centred * centred, axis=0, keepdims=True) + EPS)
        inv_in[:, lanes] = inv
        xn[:, lanes] = (0.5 * (centred * inv)).astype(BF16)

    live = live_row(meta, col)
    square = (TILE, TILE)
    causal = lax.broadcasted_iota(jnp.int32, square, 0) <= lax.broadcasted_iota(jnp.int32, square, 1)

    def one_head(h):
        silu, slope = silu_parts(nn(win[h], xn[...]))
        slopes[h] = slope.astype(BF16)
        rounded = silu.astype(BF16)
        proj[h] = rounded
        scores = []
        for i in range(2):
            low = i * SLOT
            key = rounded[3 * DH :, low : low + SLOT] * BF16(0.5 * DH**-0.5)
            query = rounded[2 * DH : 3 * DH, low : low + SLOT]
            both = tn(key[:, :TILE], query)
            scores.append((both[:, :TILE], both[:, TILE:], tn(key[:, TILE:], query[:, TILE:])))
        parts = []
        for i in range(2):
            low = i * SLOT
            value = rounded[DH : 2 * DH, low : low + SLOT]
            held = []
            for at, half in enumerate(scores[i]):
                weight, slope = silu_parts(half)
                if at != 1:
                    weight = jnp.where(causal, weight, 0.0)
                    slope = jnp.where(causal, slope, 0.0)
                lanes = slice(at * TILE, (at + 1) * TILE)
                held.append(weight.astype(BF16))
                weights[h, i, :, lanes] = held[at]
                score_slopes[h, i, :, lanes] = slope.astype(BF16)
            first = nn(value[:, :TILE], jnp.concatenate(held[:2], axis=1))
            parts += [first[:, :TILE], first[:, TILE:] + nn(value[:, TILE:], held[2])]
        att = jnp.concatenate(parts, axis=1) * live
        out_norm[pl.ds(pl.multiple_of(h * DH, DH), DH), :] = att
        return att

    def head_step(z, sums):
        for h in (2 * z, 2 * z + 1):
            att = one_head(h)
            sums = (
                sums[0] + jnp.sum(att, axis=0, keepdims=True),
                sums[1] + jnp.sum(att * att, axis=0, keepdims=True),
            )
        return sums

    zero = jnp.zeros((1, tokens), F32)
    totals, squares = lax.fori_loop(0, H // 2, head_step, (zero, zero), unroll=True)
    mean = totals / D
    inv = lax.rsqrt(squares / D - mean * mean + EPS)
    inv_out[...] = inv

    def gate_step(h, carry):
        rows = pl.ds(h * DH, DH)
        normed = (out_norm[rows, :] - mean) * inv
        out_norm[rows, :] = normed
        gated[rows, :] = (normed * proj[h, :DH, :].astype(F32)).astype(BF16)
        return carry

    lax.fori_loop(0, H, gate_step, 0, unroll=4)
    out = (x_s[...] + tn(wout[...], gated[...])).astype(BF16)
    for i in range(2):
        mixed[:, i] = out[:, i * SLOT : (i + 1) * SLOT].reshape(H, DH, SLOT)
    split_chunks(place, mixed, msame, mcross)


def backward_kernel(
    place,
    meta,
    gy_ref,
    win,
    wout,
    xn,
    inv_in,
    slopes,
    proj,
    weights,
    score_slopes,
    out_norm,
    inv_out,
    gated,
    gfeat,
    mine,
    other,
    grad_s,
    gy_s,
    gpre_s,
    sum_s,
    gwo_s,
):
    tokens = 2 * SLOT
    core = place[1]
    for i in range(2):
        gy_s[:, i * SLOT : (i + 1) * SLOT] = gy_ref[i]
    grad_s[...] = nn(wout[...], gy_s[...])
    gwo_s[...] = nt(gated[...], gy_s[...]).astype(BF16)

    def sum_step(h, sums):
        rows = pl.ds(h * DH, DH)
        grad = grad_s[rows, :] * proj[h, :DH, :].astype(F32)
        return (
            sums[0] + jnp.sum(grad, axis=0, keepdims=True),
            sums[1] + jnp.sum(grad * out_norm[rows, :], axis=0, keepdims=True),
        )

    zero = jnp.zeros((1, tokens), F32)
    first, second = lax.fori_loop(0, H, sum_step, (zero, zero), unroll=4)
    first = first / D
    second = second / D
    inv = inv_out[...] * live_row(meta, place[0])

    def store_grad(ref, at, grad_win, grad_wout):
        for part in range(4):
            lanes = slice(part * 128, (part + 1) * 128)
            for c in range(4):
                ref[4 * part + c, at, :DH, :] = grad_win[c * DH : (c + 1) * DH, lanes]
                ref[4 * part + c, at, DH:, :] = grad_wout[c * DH // 4 : (c + 1) * DH // 4, lanes]

    def one_head(h):
        rows = pl.ds(pl.multiple_of(h * DH, DH), DH)
        grad_gated = grad_s[rows, :]
        normed = out_norm[rows, :]
        grad_normo = grad_gated * proj[h, :DH, :].astype(F32)
        grad_att = (inv * (grad_normo - first - normed * second)).astype(BF16)
        grads = ([], [], [])
        for i in range(2):
            low = i * SLOT
            lanes = slice(low, low + SLOT)
            value = proj[h, DH : 2 * DH, lanes]
            query = proj[h, 2 * DH : 3 * DH, lanes] * BF16(0.5 * DH**-0.5)
            key = proj[h, 3 * DH :, lanes] * BF16(0.5 * DH**-0.5)
            grad = grad_att[:, lanes]
            scores = tn(value[:, :TILE], grad) * score_slopes[h, i, :, :SLOT].astype(F32)
            scores = scores.astype(BF16)
            tail = tn(value[:, TILE:], grad[:, TILE:]) * score_slopes[h, i, :, SLOT:].astype(F32)
            tail = tail.astype(BF16)
            grad_query = nn(key[:, :TILE], scores)
            grads[0].append(nt(grad, weights[h, i, :, :SLOT]))
            grads[0].append(nt(grad[:, TILE:], weights[h, i, :, SLOT:]))
            grads[1].append(grad_query[:, :TILE])
            grads[1].append(grad_query[:, TILE:] + nn(key[:, TILE:], tail))
            grads[2].append(nt(query, scores))
            grads[2].append(nt(query[:, TILE:], tail))
        stacked = [grad_gated * normed] + [jnp.concatenate(blocks, axis=1) for blocks in grads]
        grad_pre = (jnp.concatenate(stacked, axis=0) * slopes[h].astype(F32)).astype(BF16)
        gpre_s[h] = grad_pre
        return nt(grad_pre, xn[...]).astype(BF16), gwo_s[rows, :]

    def head_step(z, carry):
        store_grad(mine, z, *one_head(2 * z + core))
        store_grad(other, z, *one_head(2 * z + 1 - core))
        return carry

    lax.fori_loop(0, H // 2, head_step, 0, unroll=True)
    sum_s[...] = tn(win[...].reshape(4 * D, D), gpre_s[...].reshape(4 * D, tokens))
    for i in range(tokens // 128):
        lanes = slice(i * 128, (i + 1) * 128)
        grad = 0.5 * sum_s[:, lanes]
        normed = 2.0 * xn[:, lanes].astype(F32)
        lead = jnp.mean(grad, axis=0, keepdims=True)
        cross = jnp.mean(grad * normed, axis=0, keepdims=True)
        total = gy_s[:, lanes].astype(F32) + inv_in[:, lanes] * (grad - lead - normed * cross)
        here = slice(i % 2 * 128, (i % 2 + 1) * 128)
        gfeat[:, i // 2, :, here] = total.astype(BF16).reshape(H, DH, 128)


def run_forward(place, meta, xa, pieces):
    tokens = 2 * SLOT
    shape = jax.ShapeDtypeStruct
    return pl.pallas_call(
        forward_kernel,
        out_shape=(
            shape((4, 2, DH, SLOT), BF16),
            shape((4, 2, DH, SLOT), BF16),
            shape((H, 4 * DH, D), BF16),
            shape((D, D), BF16),
            shape((D, tokens), BF16),
            shape((1, tokens), F32),
            shape((H, 4 * DH, tokens), BF16),
            shape((H, 4 * DH, tokens), BF16),
            shape((H, 2, TILE, 3 * TILE), BF16),
            shape((H, 2, TILE, 3 * TILE), BF16),
            shape((D, tokens), F32),
            shape((1, tokens), F32),
            shape((D, tokens), BF16),
        ),
        in_specs=[SMEM, SMEM] + [VMEM] * 9,
        out_specs=(VMEM,) * 13,
        scratch_shapes=[pltpu.VMEM((H, 2, DH, SLOT), BF16), pltpu.VMEM((D, tokens), F32)],
        compiler_params=params(28),
        cost_estimate=cost(10**10, 2**24),
    )(place, meta, xa, *pieces)


def run_backward(place, meta, grad_y, saved):
    tokens = 2 * SLOT
    piece = jax.ShapeDtypeStruct((16, 4, PIECE, 128), BF16)
    return pl.pallas_call(
        backward_kernel,
        out_shape=(jax.ShapeDtypeStruct((H, 2, DH, SLOT), BF16), piece, piece),
        in_specs=[SMEM, SMEM] + [VMEM] * 12,
        out_specs=(VMEM,) * 3,
        cost_estimate=cost(12 * 10**9, 2**24),
        scratch_shapes=[
            pltpu.VMEM((D, tokens), F32),
            pltpu.VMEM((D, tokens), BF16),
            pltpu.VMEM((H, 4 * DH, tokens), BF16),
            pltpu.VMEM((D, tokens), F32),
            pltpu.VMEM((D, D), BF16),
        ],
        compiler_params=params(32),
    )(place, meta, grad_y, *saved)


def finish_kernel(arrived, grad_in, grad_out):
    factor = float(HIST * 32 * SLOT) ** -0.5
    for part in range(4):
        lanes = slice(part * 128, (part + 1) * 128)
        for c in range(4):
            block = arrived[4 * part + c].astype(F32) * factor
            grad_in[c, :, lanes] = block[:DH]
            grad_out[c * DH // 4 : (c + 1) * DH // 4, lanes] = block[DH:]


def shift(x, axis, k):
    return lax.ppermute(x, axis, [(i, (i + k) % 4) for i in range(4)])


def trade(x, axis):
    return lax.ppermute(x, axis, [(0, 1), (1, 0)])


def turn(part, k, flip):
    pairs = []
    for y in range(4):
        for x in range(4):
            for core in range(2):
                goal = 4 * y + (x + k) % 4 if core == flip else 4 * ((y + k) % 4) + x
                pairs.append(((4 * y + x) * 2 + core, goal * 2 + core))
    return lax.ppermute(part, ("y", "x", "core"), pairs)


def gather_weights(shards):
    own = [jnp.stack(shards)]
    own += [turn(own[0], k, 0) for k in range(1, 4)]
    return own + [trade(part, "core") for part in own]


def swap(x, axes):
    return lax.all_to_all(x, axes, split_axis=0, concat_axis=0, tiled=True)


def on_device(features, cotangent, lengths, route, w_in, w_out):
    groups = lax.axis_size(DP)
    col = lax.axis_index(COL)
    core = lax.axis_index("core")
    zhi = lax.axis_index("zhi")
    route = route.T
    x = lax.axis_index("x")
    y = lax.axis_index("y")
    along = jnp.where(core == 0, x, y)
    place = jnp.stack([col, core, zhi, along, x + y - along]).astype(jnp.int32)

    sent, piece = pl.pallas_call(
        spread_kernel,
        out_shape=(
            jax.ShapeDtypeStruct((groups, DH + META, SLOT), BF16),
            jax.ShapeDtypeStruct((PIECE, D), BF16),
        ),
        in_specs=[SMEM, SMEM, SMEM, VMEM, VMEM, VMEM],
        out_specs=(VMEM, VMEM),
        compiler_params=params(16),
    )(place, route, lengths, features, w_in.transpose(0, 2, 1), w_out)
    arrived = swap(sent, DP)
    shards = [piece] + [shift(piece, "zhi", k) for k in range(1, 4)]
    rows, meta = pl.pallas_call(
        settle_kernel,
        out_shape=(
            jax.ShapeDtypeStruct((HIST, DH, SLOT), BF16),
            jax.ShapeDtypeStruct((2, HIST), jnp.int32),
        ),
        in_specs=[VMEM, ANY, ANY, ANY],
        out_specs=(VMEM, SMEM),
        compiler_params=params(16),
    )(arrived, *shards[1:])
    pieces = gather_weights(shards)
    xa = swap(rows, COL).reshape(H, 2, DH, SLOT)
    grad_y = lax.dynamic_slice_in_dim(cotangent, 2 * col, 2, 0)
    msame, mcross, *saved = run_forward(place, meta, xa, pieces)
    gfeat, mine, other = run_backward(place, meta, grad_y, saved)
    home = swap(gfeat.reshape(HIST, DH, SLOT), COL)

    def local(kernel, outs, *args):
        return pl.pallas_call(
            kernel,
            out_shape=outs,
            in_specs=[SMEM] + [VMEM] * (len(args) - 1),
            out_specs=(VMEM,) * len(outs),
            compiler_params=params(16),
        )(*args)

    part = jax.ShapeDtypeStruct((4, 4, PIECE, 128), BF16)
    sums = local(add_kernel, (part,) * 4, place, mine, trade(other, "core"))
    came = [turn(sums[k], k, 0) for k in range(1, 4)]
    part = jax.ShapeDtypeStruct((4, PIECE, 128), BF16)
    sums = local(cross_kernel, (part,) * 4, place, sums[0], *came)
    gate1 = sums[1]
    came = [turn(sums[k], k, 1) for k in range(1, 4)]
    part = jax.ShapeDtypeStruct((PIECE, 128), BF16)
    kept = jax.ShapeDtypeStruct((PIECE, 128), F32)
    sums = local(depth_kernel, (kept,) + (part,) * 3, place, sums[0], *came)
    gate2 = sums[1]
    came = [shift(sums[k], "zhi", k) for k in range(1, 4)]
    total, rounded = pl.pallas_call(
        last_kernel,
        out_shape=(kept, part),
        in_specs=[VMEM] * 4,
        out_specs=(VMEM, VMEM),
        compiler_params=params(16),
    )(sums[0], *came)

    def col_pairs(same, cross, after):
        pair = jax.ShapeDtypeStruct((2, 2, DH, SLOT), BF16)
        pairs = pl.pallas_call(
            pair_kernel,
            out_shape=(pair,) * 4,
            in_specs=[VMEM, VMEM, ANY],
            out_specs=(VMEM,) * 4,
            compiler_params=params(16),
        )(same, trade(cross, "core"), after)
        return [pairs[0]] + [shift(pairs[k], "zhi", k) for k in range(1, 4)]

    back = pl.pallas_call(
        return_kernel,
        out_shape=jax.ShapeDtypeStruct((groups, DH, SLOT), BF16),
        in_specs=[SMEM, VMEM, ANY],
        out_specs=VMEM,
        compiler_params=params(16),
    )(meta, home, gate2)
    arrived = swap(back, DP)
    moved = col_pairs(msame, mcross, rounded)
    block = jax.ShapeDtypeStruct((HIST, DH, SLOT), BF16)
    grad_features, mixed = pl.pallas_call(
        collect_kernel,
        out_shape=(block, block),
        in_specs=[SMEM, SMEM] + [VMEM] * 5,
        out_specs=(VMEM, VMEM),
        compiler_params=params(16),
    )(place, route, arrived, *moved)

    whole = pl.pallas_call(
        repeat_kernel,
        out_shape=jax.ShapeDtypeStruct((16, PIECE, 128), BF16),
        in_specs=[VMEM, VMEM, ANY],
        out_specs=VMEM,
        compiler_params=params(16),
    )(total, trade(rounded, "zlo"), arrived)
    whole = swap(whole, ("y", "x"))
    grad_in, grad_out = pl.pallas_call(
        finish_kernel,
        out_shape=(jax.ShapeDtypeStruct((4, DH, D), F32), jax.ShapeDtypeStruct((DH, D), F32)),
        in_specs=[VMEM],
        out_specs=(VMEM, VMEM),
        compiler_params=params(16),
    )(whole)
    return (mixed, grad_features, grad_in.transpose(0, 2, 1), grad_out)


def solution(mesh):
    split = Mesh(mesh.devices.reshape(4, 4, 2, 4, 2), ("y", "x", "zlo", "zhi", "core"))
    in_specs = (P(DP, COL, None), P(DP, None, None), P(DP), P(DP, None), P(None, None, COL), P(COL, None))
    out_specs = (P(DP, COL, None), P(DP, COL, None), P(None, None, COL), P(COL, None))
    return jax.shard_map(
        on_device, mesh=split, in_specs=in_specs, out_specs=out_specs, check_vma=False
    )
```

```python
import jax
import jax.numpy as jnp
from jax import lax
from jax.experimental import pallas as pl
from jax.experimental.pallas import tpu as pltpu
from jax.sharding import Mesh
from jax.sharding import PartitionSpec as P

D = 512
H = 8
DH = 64
SLOT = 256
HIST = 16
EPS = 1e-05
META = 16
TILE = 128
ROWS = 5 * DH
PIECE = ROWS // 4
F32 = jnp.float32
BF16 = jnp.bfloat16
DP = ("y", "x", "zlo")
COL = ("zhi", "core")
VMEM = pl.BlockSpec(memory_space=pltpu.VMEM)
SMEM = pl.BlockSpec(memory_space=pltpu.SMEM)
ANY = pl.BlockSpec(memory_space=pl.ANY)


def params(mib):
    return pltpu.CompilerParams(vmem_limit_bytes=mib * 1024 * 1024)


def cost(flops, moved):
    return pl.CostEstimate(flops=flops, bytes_accessed=moved, transcendentals=0)


def spread_kernel(place, route, lengths, rows, proj, wout, sent, piece, rows_s, sems):
    along = place[3]
    wrows = pl.ds(pl.multiple_of(along * (DH // 4), DH // 4), DH // 4)
    copies = (
        pltpu.make_async_copy(proj.at[along], piece.at[pl.ds(0, DH)], sems.at[0]),
        pltpu.make_async_copy(wout.at[wrows], piece.at[pl.ds(DH, DH // 4)], sems.at[1]),
        pltpu.make_async_copy(rows, rows_s, sems.at[2]),
    )
    for copy in copies:
        copy.start()
    sent[...] = jnp.zeros_like(sent)
    for copy in copies:
        copy.wait()
    for h in range(HIST):
        group = route[0, h]
        sent[group, :DH, :] = rows_s[h, :, :TILE]
        sent[group, DH : 2 * DH, :] = rows_s[h, :, TILE:]
        slot = (route[1, h] + 1).astype(F32)
        count = lengths[h].astype(F32)
        note = jnp.concatenate([jnp.full((8, TILE), slot, F32), jnp.full((8, TILE), count, F32)], axis=0)
        sent[group, 2 * DH :, :] = note.astype(BF16)


def settle_kernel(arrived, shard1, shard2, shard3, rows, meta):
    codes = []
    for group in range(arrived.shape[0]):
        note = arrived[group, 2 * DH :, :].astype(F32)
        code = jnp.max(note[:8] * 512.0 + note[8:])
        codes.append(code.astype(jnp.int32))
    for group, code in enumerate(codes):

        @pl.when(code >= 512)
        def _():
            slot = lax.shift_right_logical(code, 9) - 1
            rows[slot, :, :TILE] = arrived[group, :DH, :]
            rows[slot, :, TILE:] = arrived[group, DH : 2 * DH, :]
            meta[0, slot] = group
            meta[1, slot] = code & 511


def add_kernel(place, mine, came, sum0, sum1, sum2, sum3):
    core = place[1]
    for k, total in enumerate((sum0, sum1, sum2, sum3)):
        ahead = lax.rem(place[3] + k, 4)
        for j in range(4):
            piece = jnp.where(core == 0, 4 * j + ahead, 4 * ahead + j)
            total[j] = (mine[piece].astype(F32) + came[piece].astype(F32)).astype(BF16)


def cross_kernel(place, kept, came1, came2, came3, sum0, sum1, sum2, sum3):
    for k, total in enumerate((sum0, sum1, sum2, sum3)):
        j = lax.rem(place[4] + k, 4)
        part = kept[j].astype(F32)
        for came in (came1, came2, came3):
            part = part + came[j].astype(F32)
        total[...] = part.astype(BF16)


def depth_kernel(place, kept, came1, came2, came3, sum0, sum1, sum2, sum3):
    for k, total in enumerate((sum0, sum1, sum2, sum3)):
        z = lax.rem(place[2] + k, 4)
        part = kept[z].astype(F32)
        for came in (came1, came2, came3):
            part = part + came[z].astype(F32)
        total[...] = part.astype(BF16) if k else part


def last_kernel(kept, came1, came2, came3, total, rounded):
    part = kept[...]
    for came in (came1, came2, came3):
        part = part + came[...].astype(F32)
    total[...] = part
    rounded[...] = part.astype(BF16)


def repeat_kernel(total, came, after, whole):
    summed = (total[...] + came[...].astype(F32)).astype(BF16)
    for group in range(whole.shape[0]):
        whole[group] = summed


def pair_kernel(same, came, after, pair0, pair1, pair2, pair3):
    for k, pair in enumerate((pair0, pair1, pair2, pair3)):
        pair[0] = same[k]
        pair[1] = came[k]


def return_kernel(meta, rows, after, sent):
    sent[...] = jnp.zeros_like(sent)
    for k in range(HIST):
        sent[meta[0, k]] = rows[k]


def collect_kernel(place, route, arrived, pair0, pair1, pair2, pair3, rows, mixed):
    for h in range(HIST):
        rows[h] = arrived[route[0, h]]
    core = place[1]
    for k, pair in enumerate((pair0, pair1, pair2, pair3)):
        for side in range(2):
            owner = 2 * wrap(place[2], k) + (core if side == 0 else 1 - core)
            for i in range(2):
                mixed[2 * owner + i] = pair[side, i]


def tn(a, b):
    return lax.dot_general(a, b, (((0,), (0,)), ((), ())), preferred_element_type=F32)


def nt(a, b):
    return lax.dot_general(a, b, (((1,), (1,)), ((), ())), preferred_element_type=F32)


def nn(a, b):
    return lax.dot_general(a, b, (((1,), (0,)), ((), ())), preferred_element_type=F32)


def silu_parts(half):
    t = jnp.tanh(half)
    up = 1.0 + t
    silu = half * up
    return silu, up + silu * (1.0 - t)


def live_row(meta, col):
    at = lax.broadcasted_iota(jnp.int32, (1, SLOT), 1)
    rows = [(at < meta[1, 2 * col + i]).astype(F32) for i in range(2)]
    return jnp.concatenate(rows, axis=1)


def wrap(position, back):
    return lax.rem(position - back + 4, 4)


def split_chunks(place, chunks, same, cross):
    for k in range(4):
        goal = 2 * lax.rem(place[2] + k, 4)
        same[k] = chunks[goal + place[1]]
        cross[k] = chunks[goal + 1 - place[1]]


def forward_kernel(
    place,
    meta,
    xa,
    own0,
    own1,
    own2,
    own3,
    far0,
    far1,
    far2,
    far3,
    msame,
    mcross,
    win,
    wout,
    xn,
    inv_in,
    slopes,
    proj,
    weights,
    score_slopes,
    out_norm,
    inv_out,
    gated,
    mixed,
    x_s,
):
    tokens = 2 * SLOT
    col = place[0]
    core = place[1]
    for i in range(2):
        x_s[:, i * SLOT : (i + 1) * SLOT] = xa[:, i].reshape(D, SLOT).astype(F32)
    for side, refs, along in ((core, (own0, own1, own2, own3), place[3]), (1 - core, (far0, far1, far2, far3), place[4])):
        for k in range(4):
            piece = wrap(along, k)
            for z in range(4):
                head = 2 * wrap(place[2], z) + side
                at = pl.multiple_of(piece * DH, DH)
                win[head, pl.ds(at, DH), :] = refs[k][z, :DH, :]
                at = pl.multiple_of(head * DH + piece * (DH // 4), DH // 4)
                wout[pl.ds(at, DH // 4), :] = refs[k][z, DH:, :]

    for i in range(tokens // 128):
        lanes = slice(i * 128, (i + 1) * 128)
        x = x_s[:, lanes]
        centred = x - jnp.mean(x, axis=0, keepdims=True)
        inv = lax.rsqrt(jnp.mean(centred * centred, axis=0, keepdims=True) + EPS)
        inv_in[:, lanes] = inv
        xn[:, lanes] = (0.5 * (centred * inv)).astype(BF16)

    live = live_row(meta, col)
    square = (TILE, TILE)
    causal = lax.broadcasted_iota(jnp.int32, square, 0) <= lax.broadcasted_iota(jnp.int32, square, 1)

    def one_head(h):
        silu, slope = silu_parts(nn(win[h], xn[...]))
        slopes[h] = slope.astype(BF16)
        rounded = silu.astype(BF16)
        proj[h] = rounded
        scores = []
        for i in range(2):
            low = i * SLOT
            key = rounded[3 * DH :, low : low + SLOT] * BF16(0.5 * DH**-0.5)
            query = rounded[2 * DH : 3 * DH, low : low + SLOT]
            both = tn(key[:, :TILE], query)
            scores.append((both[:, :TILE], both[:, TILE:], tn(key[:, TILE:], query[:, TILE:])))
        parts = []
        for i in range(2):
            low = i * SLOT
            value = rounded[DH : 2 * DH, low : low + SLOT]
            held = []
            for at, half in enumerate(scores[i]):
                weight, slope = silu_parts(half)
                if at != 1:
                    weight = jnp.where(causal, weight, 0.0)
                    slope = jnp.where(causal, slope, 0.0)
                lanes = slice(at * TILE, (at + 1) * TILE)
                held.append(weight.astype(BF16))
                weights[h, i, :, lanes] = held[at]
                score_slopes[h, i, :, lanes] = slope.astype(BF16)
            first = nn(value[:, :TILE], jnp.concatenate(held[:2], axis=1))
            parts += [first[:, :TILE], first[:, TILE:] + nn(value[:, TILE:], held[2])]
        att = jnp.concatenate(parts, axis=1) * live
        out_norm[pl.ds(pl.multiple_of(h * DH, DH), DH), :] = att
        return att

    def head_step(z, sums):
        for h in (2 * z, 2 * z + 1):
            att = one_head(h)
            sums = (
                sums[0] + jnp.sum(att, axis=0, keepdims=True),
                sums[1] + jnp.sum(att * att, axis=0, keepdims=True),
            )
        return sums

    zero = jnp.zeros((1, tokens), F32)
    totals, squares = lax.fori_loop(0, H // 2, head_step, (zero, zero), unroll=True)
    mean = totals / D
    inv = lax.rsqrt(squares / D - mean * mean + EPS)
    inv_out[...] = inv

    def gate_step(h, carry):
        rows = pl.ds(h * DH, DH)
        normed = (out_norm[rows, :] - mean) * inv
        out_norm[rows, :] = normed
        gated[rows, :] = (normed * proj[h, :DH, :].astype(F32)).astype(BF16)
        return carry

    lax.fori_loop(0, H, gate_step, 0, unroll=4)
    out = (x_s[...] + tn(wout[...], gated[...])).astype(BF16)
    for i in range(2):
        mixed[:, i] = out[:, i * SLOT : (i + 1) * SLOT].reshape(H, DH, SLOT)
    split_chunks(place, mixed, msame, mcross)


def backward_kernel(
    place,
    meta,
    gy_ref,
    win,
    wout,
    xn,
    inv_in,
    slopes,
    proj,
    weights,
    score_slopes,
    out_norm,
    inv_out,
    gated,
    gfeat,
    mine,
    other,
    grad_s,
    gy_s,
    gpre_s,
    sum_s,
    gwo_s,
):
    tokens = 2 * SLOT
    core = place[1]
    for i in range(2):
        gy_s[:, i * SLOT : (i + 1) * SLOT] = gy_ref[i]
    grad_s[...] = nn(wout[...], gy_s[...])
    gwo_s[...] = nt(gated[...], gy_s[...]).astype(BF16)

    def sum_step(h, sums):
        rows = pl.ds(h * DH, DH)
        grad = grad_s[rows, :] * proj[h, :DH, :].astype(F32)
        return (
            sums[0] + jnp.sum(grad, axis=0, keepdims=True),
            sums[1] + jnp.sum(grad * out_norm[rows, :], axis=0, keepdims=True),
        )

    zero = jnp.zeros((1, tokens), F32)
    first, second = lax.fori_loop(0, H, sum_step, (zero, zero), unroll=4)
    first = first / D
    second = second / D
    inv = inv_out[...] * live_row(meta, place[0])

    def store_grad(ref, at, grad_win, grad_wout):
        for part in range(4):
            lanes = slice(part * 128, (part + 1) * 128)
            for c in range(4):
                ref[4 * part + c, at, :DH, :] = grad_win[c * DH : (c + 1) * DH, lanes]
                ref[4 * part + c, at, DH:, :] = grad_wout[c * DH // 4 : (c + 1) * DH // 4, lanes]

    def one_head(h):
        rows = pl.ds(pl.multiple_of(h * DH, DH), DH)
        grad_gated = grad_s[rows, :]
        normed = out_norm[rows, :]
        grad_normo = grad_gated * proj[h, :DH, :].astype(F32)
        grad_att = (inv * (grad_normo - first - normed * second)).astype(BF16)
        grads = ([], [], [])
        for i in range(2):
            low = i * SLOT
            lanes = slice(low, low + SLOT)
            value = proj[h, DH : 2 * DH, lanes]
            query = proj[h, 2 * DH : 3 * DH, lanes] * BF16(0.5 * DH**-0.5)
            key = proj[h, 3 * DH :, lanes] * BF16(0.5 * DH**-0.5)
            grad = grad_att[:, lanes]
            scores = tn(value[:, :TILE], grad) * score_slopes[h, i, :, :SLOT].astype(F32)
            scores = scores.astype(BF16)
            tail = tn(value[:, TILE:], grad[:, TILE:]) * score_slopes[h, i, :, SLOT:].astype(F32)
            tail = tail.astype(BF16)
            grad_query = nn(key[:, :TILE], scores)
            grads[0].append(nt(grad, weights[h, i, :, :SLOT]))
            grads[0].append(nt(grad[:, TILE:], weights[h, i, :, SLOT:]))
            grads[1].append(grad_query[:, :TILE])
            grads[1].append(grad_query[:, TILE:] + nn(key[:, TILE:], tail))
            grads[2].append(nt(query, scores))
            grads[2].append(nt(query[:, TILE:], tail))
        stacked = [grad_gated * normed] + [jnp.concatenate(blocks, axis=1) for blocks in grads]
        grad_pre = (jnp.concatenate(stacked, axis=0) * slopes[h].astype(F32)).astype(BF16)
        gpre_s[h] = grad_pre
        return nt(grad_pre, xn[...]).astype(BF16), gwo_s[rows, :]

    def head_step(z, carry):
        store_grad(mine, z, *one_head(2 * z + core))
        store_grad(other, z, *one_head(2 * z + 1 - core))
        return carry

    lax.fori_loop(0, H // 2, head_step, 0, unroll=True)
    sum_s[...] = tn(win[...].reshape(4 * D, D), gpre_s[...].reshape(4 * D, tokens))
    for i in range(tokens // 128):
        lanes = slice(i * 128, (i + 1) * 128)
        grad = 0.5 * sum_s[:, lanes]
        normed = 2.0 * xn[:, lanes].astype(F32)
        lead = jnp.mean(grad, axis=0, keepdims=True)
        cross = jnp.mean(grad * normed, axis=0, keepdims=True)
        total = gy_s[:, lanes].astype(F32) + inv_in[:, lanes] * (grad - lead - normed * cross)
        here = slice(i % 2 * 128, (i % 2 + 1) * 128)
        gfeat[:, i // 2, :, here] = total.astype(BF16).reshape(H, DH, 128)


def run_forward(place, meta, xa, pieces):
    tokens = 2 * SLOT
    shape = jax.ShapeDtypeStruct
    return pl.pallas_call(
        forward_kernel,
        out_shape=(
            shape((4, 2, DH, SLOT), BF16),
            shape((4, 2, DH, SLOT), BF16),
            shape((H, 4 * DH, D), BF16),
            shape((D, D), BF16),
            shape((D, tokens), BF16),
            shape((1, tokens), F32),
            shape((H, 4 * DH, tokens), BF16),
            shape((H, 4 * DH, tokens), BF16),
            shape((H, 2, TILE, 3 * TILE), BF16),
            shape((H, 2, TILE, 3 * TILE), BF16),
            shape((D, tokens), F32),
            shape((1, tokens), F32),
            shape((D, tokens), BF16),
        ),
        in_specs=[SMEM, SMEM] + [VMEM] * 9,
        out_specs=(VMEM,) * 13,
        scratch_shapes=[pltpu.VMEM((H, 2, DH, SLOT), BF16), pltpu.VMEM((D, tokens), F32)],
        compiler_params=params(10),
        cost_estimate=cost(10**10, 2**24),
    )(place, meta, xa, *pieces)


def run_backward(place, meta, grad_y, saved):
    tokens = 2 * SLOT
    piece = jax.ShapeDtypeStruct((16, 4, PIECE, 128), BF16)
    return pl.pallas_call(
        backward_kernel,
        out_shape=(jax.ShapeDtypeStruct((H, 2, DH, SLOT), BF16), piece, piece),
        in_specs=[SMEM, SMEM] + [VMEM] * 12,
        out_specs=(VMEM,) * 3,
        cost_estimate=cost(12 * 10**9, 2**24),
        scratch_shapes=[
            pltpu.VMEM((D, tokens), F32),
            pltpu.VMEM((D, tokens), BF16),
            pltpu.VMEM((H, 4 * DH, tokens), BF16),
            pltpu.VMEM((D, tokens), F32),
            pltpu.VMEM((D, D), BF16),
        ],
        compiler_params=params(14),
    )(place, meta, grad_y, *saved)


def finish_kernel(arrived, grad_in, grad_out):
    factor = float(HIST * 32 * SLOT) ** -0.5
    for part in range(4):
        lanes = slice(part * 128, (part + 1) * 128)
        for c in range(4):
            block = arrived[4 * part + c].astype(F32) * factor
            grad_in[c, :, lanes] = block[:DH]
            grad_out[c * DH // 4 : (c + 1) * DH // 4, lanes] = block[DH:]


def shift(x, axis, k):
    return lax.ppermute(x, axis, [(i, (i + k) % 4) for i in range(4)])


def trade(x, axis):
    return lax.ppermute(x, axis, [(0, 1), (1, 0)])


def turn(part, k, flip):
    pairs = []
    for y in range(4):
        for x in range(4):
            for core in range(2):
                goal = 4 * y + (x + k) % 4 if core == flip else 4 * ((y + k) % 4) + x
                pairs.append(((4 * y + x) * 2 + core, goal * 2 + core))
    return lax.ppermute(part, ("y", "x", "core"), pairs)


def gather_weights(shards):
    own = [jnp.stack(shards)]
    own += [turn(own[0], k, 0) for k in range(1, 4)]
    return own + [trade(part, "core") for part in own]


def swap(x, axes):
    return lax.all_to_all(x, axes, split_axis=0, concat_axis=0, tiled=True)


def on_device(features, cotangent, lengths, route, w_in, w_out):
    groups = lax.axis_size(DP)
    col = lax.axis_index(COL)
    core = lax.axis_index("core")
    zhi = lax.axis_index("zhi")
    route = route.T
    x = lax.axis_index("x")
    y = lax.axis_index("y")
    along = jnp.where(core == 0, x, y)
    place = jnp.stack([col, core, zhi, along, x + y - along]).astype(jnp.int32)

    sent, piece = pl.pallas_call(
        spread_kernel,
        out_shape=(
            jax.ShapeDtypeStruct((groups, 2 * DH + META, TILE), BF16),
            jax.ShapeDtypeStruct((PIECE, D), BF16),
        ),
        in_specs=[SMEM, SMEM, SMEM, ANY, ANY, ANY],
        out_specs=(VMEM, VMEM),
        scratch_shapes=[pltpu.VMEM((HIST, DH, SLOT), BF16), pltpu.SemaphoreType.DMA((3,))],
        compiler_params=params(60),
    )(place, route, lengths, features, w_in.transpose(0, 2, 1), w_out)
    arrived = swap(sent, DP)
    shards = [piece] + [shift(piece, "zhi", k) for k in range(1, 4)]
    rows, meta = pl.pallas_call(
        settle_kernel,
        out_shape=(
            jax.ShapeDtypeStruct((HIST, DH, SLOT), BF16),
            jax.ShapeDtypeStruct((2, HIST), jnp.int32),
        ),
        in_specs=[VMEM, ANY, ANY, ANY],
        out_specs=(VMEM, SMEM),
        compiler_params=params(6),
    )(arrived, *shards[1:])
    pieces = gather_weights(shards)
    xa = swap(rows, COL).reshape(H, 2, DH, SLOT)
    grad_y = lax.dynamic_slice_in_dim(cotangent, 2 * col, 2, 0)
    msame, mcross, *saved = run_forward(place, meta, xa, pieces)
    gfeat, mine, other = run_backward(place, meta, grad_y, saved)
    home = swap(gfeat.reshape(HIST, DH, SLOT), COL)

    def local(kernel, outs, *args):
        return pl.pallas_call(
            kernel,
            out_shape=outs,
            in_specs=[SMEM] + [VMEM] * (len(args) - 1),
            out_specs=(VMEM,) * len(outs),
            compiler_params=params(6),
        )(*args)

    part = jax.ShapeDtypeStruct((4, 4, PIECE, 128), BF16)
    sums = local(add_kernel, (part,) * 4, place, mine, trade(other, "core"))
    came = [turn(sums[k], k, 0) for k in range(1, 4)]
    part = jax.ShapeDtypeStruct((4, PIECE, 128), BF16)
    sums = local(cross_kernel, (part,) * 4, place, sums[0], *came)
    gate1 = sums[1]
    came = [turn(sums[k], k, 1) for k in range(1, 4)]
    part = jax.ShapeDtypeStruct((PIECE, 128), BF16)
    kept = jax.ShapeDtypeStruct((PIECE, 128), F32)
    sums = local(depth_kernel, (kept,) + (part,) * 3, place, sums[0], *came)
    gate2 = sums[1]
    came = [shift(sums[k], "zhi", k) for k in range(1, 4)]
    total, rounded = pl.pallas_call(
        last_kernel,
        out_shape=(kept, part),
        in_specs=[VMEM] * 4,
        out_specs=(VMEM, VMEM),
        compiler_params=params(6),
    )(sums[0], *came)

    def col_pairs(same, cross, after):
        pair = jax.ShapeDtypeStruct((2, 2, DH, SLOT), BF16)
        pairs = pl.pallas_call(
            pair_kernel,
            out_shape=(pair,) * 4,
            in_specs=[VMEM, VMEM, ANY],
            out_specs=(VMEM,) * 4,
            compiler_params=params(6),
        )(same, trade(cross, "core"), after)
        return [pairs[0]] + [shift(pairs[k], "zhi", k) for k in range(1, 4)]

    back = pl.pallas_call(
        return_kernel,
        out_shape=jax.ShapeDtypeStruct((groups, DH, SLOT), BF16),
        in_specs=[SMEM, VMEM, ANY],
        out_specs=VMEM,
        compiler_params=params(6),
    )(meta, home, gate2)
    arrived = swap(back, DP)
    moved = col_pairs(msame, mcross, rounded)
    block = jax.ShapeDtypeStruct((HIST, DH, SLOT), BF16)
    grad_features, mixed = pl.pallas_call(
        collect_kernel,
        out_shape=(block, block),
        in_specs=[SMEM, SMEM] + [VMEM] * 5,
        out_specs=(VMEM, VMEM),
        compiler_params=params(6),
    )(place, route, arrived, *moved)

    whole = pl.pallas_call(
        repeat_kernel,
        out_shape=jax.ShapeDtypeStruct((16, PIECE, 128), BF16),
        in_specs=[VMEM, VMEM, ANY],
        out_specs=VMEM,
        compiler_params=params(6),
    )(total, trade(rounded, "zlo"), arrived)
    whole = swap(whole, ("y", "x"))
    grad_in, grad_out = pl.pallas_call(
        finish_kernel,
        out_shape=(jax.ShapeDtypeStruct((4, DH, D), F32), jax.ShapeDtypeStruct((DH, D), F32)),
        in_specs=[VMEM],
        out_specs=(VMEM, VMEM),
        compiler_params=params(6),
    )(whole)
    return (mixed, grad_features, grad_in.transpose(0, 2, 1), grad_out)


def solution(mesh):
    split = Mesh(mesh.devices.reshape(4, 4, 2, 4, 2), ("y", "x", "zlo", "zhi", "core"))
    in_specs = (P(DP, COL, None), P(DP, None, None), P(DP), P(DP, None), P(None, None, COL), P(COL, None))
    out_specs = (P(DP, COL, None), P(DP, COL, None), P(None, None, COL), P(COL, None))
    return jax.shard_map(
        on_device, mesh=split, in_specs=in_specs, out_specs=out_specs, check_vma=False
    )
```

```python
import jax
import jax.numpy as jnp
from jax import lax
from jax.experimental import pallas as pl
from jax.experimental.pallas import tpu as pltpu
from jax.sharding import Mesh
from jax.sharding import PartitionSpec as P

D = 512
H = 8
DH = 64
SLOT = 256
HIST = 16
EPS = 1e-05
META = 16
TILE = 128
ROWS = 5 * DH
PIECE = ROWS // 4
F32 = jnp.float32
BF16 = jnp.bfloat16
DP = ("y", "x", "zlo")
COL = ("zhi", "core")
VMEM = pl.BlockSpec(memory_space=pltpu.VMEM)
SMEM = pl.BlockSpec(memory_space=pltpu.SMEM)
ANY = pl.BlockSpec(memory_space=pl.ANY)


def params(mib):
    return pltpu.CompilerParams(vmem_limit_bytes=mib * 1024 * 1024)


def cost(flops, moved):
    return pl.CostEstimate(flops=flops, bytes_accessed=moved, transcendentals=0)


def spread_kernel(route, lengths, rows, proj, wout, sent, piece, rows_s, sems):
    along = jnp.where(lax.axis_index("core") == 0, lax.axis_index("x"), lax.axis_index("y"))
    wrows = pl.ds(pl.multiple_of(along * (DH // 4), DH // 4), DH // 4)
    copies = (
        pltpu.make_async_copy(proj.at[along], piece.at[pl.ds(0, DH)], sems.at[0]),
        pltpu.make_async_copy(wout.at[wrows], piece.at[pl.ds(DH, DH // 4)], sems.at[1]),
        pltpu.make_async_copy(rows, rows_s, sems.at[2]),
    )
    for copy in copies:
        copy.start()
    sent[...] = jnp.zeros_like(sent)
    for copy in copies:
        copy.wait()
    for h in range(HIST):
        group = route[0, h]
        sent[group, :DH, :] = rows_s[h, :, :TILE]
        sent[group, DH : 2 * DH, :] = rows_s[h, :, TILE:]
        slot = (route[1, h] + 1).astype(F32)
        count = lengths[h].astype(F32)
        note = jnp.concatenate([jnp.full((8, TILE), slot, F32), jnp.full((8, TILE), count, F32)], axis=0)
        sent[group, 2 * DH :, :] = note.astype(BF16)


def settle_kernel(arrived, shard1, shard2, shard3, rows, meta):
    codes = []
    for group in range(arrived.shape[0]):
        note = arrived[group, 2 * DH :, :].astype(F32)
        code = jnp.max(note[:8] * 512.0 + note[8:])
        codes.append(code.astype(jnp.int32))
    for group, code in enumerate(codes):

        @pl.when(code >= 512)
        def _():
            slot = lax.shift_right_logical(code, 9) - 1
            rows[slot, :, :TILE] = arrived[group, :DH, :]
            rows[slot, :, TILE:] = arrived[group, DH : 2 * DH, :]
            meta[0, slot] = group
            meta[1, slot] = code & 511


def add_kernel(place, mine, came, sum0, sum1, sum2, sum3):
    core = place[1]
    for k, total in enumerate((sum0, sum1, sum2, sum3)):
        ahead = lax.rem(place[3] + k, 4)
        for j in range(4):
            piece = jnp.where(core == 0, 4 * j + ahead, 4 * ahead + j)
            total[j] = (mine[piece].astype(F32) + came[piece].astype(F32)).astype(BF16)


def cross_kernel(place, kept, came1, came2, came3, sum0, sum1, sum2, sum3):
    for k, total in enumerate((sum0, sum1, sum2, sum3)):
        j = lax.rem(place[4] + k, 4)
        part = kept[j].astype(F32)
        for came in (came1, came2, came3):
            part = part + came[j].astype(F32)
        total[...] = part.astype(BF16)


def depth_kernel(place, kept, came1, came2, came3, sum0, sum1, sum2, sum3):
    for k, total in enumerate((sum0, sum1, sum2, sum3)):
        z = lax.rem(place[2] + k, 4)
        part = kept[z].astype(F32)
        for came in (came1, came2, came3):
            part = part + came[z].astype(F32)
        total[...] = part.astype(BF16) if k else part


def last_kernel(kept, came1, came2, came3, total, rounded):
    part = kept[...]
    for came in (came1, came2, came3):
        part = part + came[...].astype(F32)
    total[...] = part
    rounded[...] = part.astype(BF16)


def repeat_kernel(total, came, after, whole):
    summed = (total[...] + came[...].astype(F32)).astype(BF16)
    for group in range(whole.shape[0]):
        whole[group] = summed


def pair_kernel(same, came, after, pair0, pair1, pair2, pair3):
    for k, pair in enumerate((pair0, pair1, pair2, pair3)):
        pair[0] = same[k]
        pair[1] = came[k]


def return_kernel(meta, rows, after, sent):
    sent[...] = jnp.zeros_like(sent)
    for k in range(HIST):
        sent[meta[0, k]] = rows[k]


def collect_kernel(route, arrived, rows):
    for h in range(HIST):
        rows[h] = arrived[route[0, h]]


def mixed_kernel(place, pair0, pair1, pair2, pair3, mixed):
    core = place[1]
    for k, pair in enumerate((pair0, pair1, pair2, pair3)):
        for side in range(2):
            owner = 2 * wrap(place[2], k) + (core if side == 0 else 1 - core)
            for i in range(2):
                mixed[2 * owner + i] = pair[side, i]


def tn(a, b):
    return lax.dot_general(a, b, (((0,), (0,)), ((), ())), preferred_element_type=F32)


def nt(a, b):
    return lax.dot_general(a, b, (((1,), (1,)), ((), ())), preferred_element_type=F32)


def nn(a, b):
    return lax.dot_general(a, b, (((1,), (0,)), ((), ())), preferred_element_type=F32)


def silu_parts(half):
    t = jnp.tanh(half)
    up = 1.0 + t
    silu = half * up
    return silu, up + silu * (1.0 - t)


def live_row(meta, col):
    at = lax.broadcasted_iota(jnp.int32, (1, SLOT), 1)
    rows = [(at < meta[1, 2 * col + i]).astype(F32) for i in range(2)]
    return jnp.concatenate(rows, axis=1)


def wrap(position, back):
    return lax.rem(position - back + 4, 4)


def split_chunks(place, chunks, same, cross):
    for k in range(4):
        goal = 2 * lax.rem(place[2] + k, 4)
        same[k] = chunks[goal + place[1]]
        cross[k] = chunks[goal + 1 - place[1]]


def forward_kernel(
    place,
    meta,
    xa,
    own0,
    own1,
    own2,
    own3,
    far0,
    far1,
    far2,
    far3,
    msame,
    mcross,
    win,
    wout,
    xn,
    inv_in,
    slopes,
    proj,
    weights,
    score_slopes,
    out_norm,
    inv_out,
    gated,
    mixed,
    x_s,
):
    tokens = 2 * SLOT
    col = place[0]
    core = place[1]
    for i in range(2):
        x_s[:, i * SLOT : (i + 1) * SLOT] = xa[:, i].reshape(D, SLOT).astype(F32)
    for side, refs, along in ((core, (own0, own1, own2, own3), place[3]), (1 - core, (far0, far1, far2, far3), place[4])):
        for k in range(4):
            piece = wrap(along, k)
            for z in range(4):
                head = 2 * wrap(place[2], z) + side
                at = pl.multiple_of(piece * DH, DH)
                win[head, pl.ds(at, DH), :] = refs[k][z, :DH, :]
                at = pl.multiple_of(head * DH + piece * (DH // 4), DH // 4)
                wout[pl.ds(at, DH // 4), :] = refs[k][z, DH:, :]

    for i in range(tokens // 128):
        lanes = slice(i * 128, (i + 1) * 128)
        x = x_s[:, lanes]
        centred = x - jnp.mean(x, axis=0, keepdims=True)
        inv = lax.rsqrt(jnp.mean(centred * centred, axis=0, keepdims=True) + EPS)
        inv_in[:, lanes] = inv
        xn[:, lanes] = (0.5 * (centred * inv)).astype(BF16)

    live = live_row(meta, col)
    square = (TILE, TILE)
    causal = lax.broadcasted_iota(jnp.int32, square, 0) <= lax.broadcasted_iota(jnp.int32, square, 1)

    def one_head(h):
        silu, slope = silu_parts(nn(win[h], xn[...]))
        slopes[h] = slope.astype(BF16)
        rounded = silu.astype(BF16)
        proj[h] = rounded
        scores = []
        for i in range(2):
            low = i * SLOT
            key = rounded[3 * DH :, low : low + SLOT] * BF16(0.5 * DH**-0.5)
            query = rounded[2 * DH : 3 * DH, low : low + SLOT]
            both = tn(key[:, :TILE], query)
            scores.append((both[:, :TILE], both[:, TILE:], tn(key[:, TILE:], query[:, TILE:])))
        parts = []
        for i in range(2):
            low = i * SLOT
            value = rounded[DH : 2 * DH, low : low + SLOT]
            held = []
            for at, half in enumerate(scores[i]):
                weight, slope = silu_parts(half)
                if at != 1:
                    weight = jnp.where(causal, weight, 0.0)
                    slope = jnp.where(causal, slope, 0.0)
                lanes = slice(at * TILE, (at + 1) * TILE)
                held.append(weight.astype(BF16))
                weights[h, i, :, lanes] = held[at]
                score_slopes[h, i, :, lanes] = slope.astype(BF16)
            first = nn(value[:, :TILE], jnp.concatenate(held[:2], axis=1))
            parts += [first[:, :TILE], first[:, TILE:] + nn(value[:, TILE:], held[2])]
        att = jnp.concatenate(parts, axis=1) * live
        out_norm[pl.ds(pl.multiple_of(h * DH, DH), DH), :] = att
        return att

    def head_step(z, sums):
        for h in (2 * z, 2 * z + 1):
            att = one_head(h)
            sums = (
                sums[0] + jnp.sum(att, axis=0, keepdims=True),
                sums[1] + jnp.sum(att * att, axis=0, keepdims=True),
            )
        return sums

    zero = jnp.zeros((1, tokens), F32)
    totals, squares = lax.fori_loop(0, H // 2, head_step, (zero, zero), unroll=True)
    mean = totals / D
    inv = lax.rsqrt(squares / D - mean * mean + EPS)
    inv_out[...] = inv

    def gate_step(h, carry):
        rows = pl.ds(h * DH, DH)
        normed = (out_norm[rows, :] - mean) * inv
        out_norm[rows, :] = normed
        gated[rows, :] = (normed * proj[h, :DH, :].astype(F32)).astype(BF16)
        return carry

    lax.fori_loop(0, H, gate_step, 0, unroll=4)
    out = (x_s[...] + tn(wout[...], gated[...])).astype(BF16)
    for i in range(2):
        mixed[:, i] = out[:, i * SLOT : (i + 1) * SLOT].reshape(H, DH, SLOT)
    split_chunks(place, mixed, msame, mcross)


def backward_kernel(
    place,
    meta,
    gy_ref,
    win,
    wout,
    xn,
    inv_in,
    slopes,
    proj,
    weights,
    score_slopes,
    out_norm,
    inv_out,
    gated,
    gfeat,
    mine,
    other,
    grad_s,
    gy_s,
    gpre_s,
    sum_s,
    gwo_s,
):
    tokens = 2 * SLOT
    core = place[1]
    for i in range(2):
        gy_s[:, i * SLOT : (i + 1) * SLOT] = gy_ref[i]
    grad_s[...] = nn(wout[...], gy_s[...])
    gwo_s[...] = nt(gated[...], gy_s[...]).astype(BF16)

    def sum_step(h, sums):
        rows = pl.ds(h * DH, DH)
        grad = grad_s[rows, :] * proj[h, :DH, :].astype(F32)
        return (
            sums[0] + jnp.sum(grad, axis=0, keepdims=True),
            sums[1] + jnp.sum(grad * out_norm[rows, :], axis=0, keepdims=True),
        )

    zero = jnp.zeros((1, tokens), F32)
    first, second = lax.fori_loop(0, H, sum_step, (zero, zero), unroll=4)
    first = first / D
    second = second / D
    inv = inv_out[...] * live_row(meta, place[0])

    def store_grad(ref, at, grad_win, grad_wout):
        for part in range(4):
            lanes = slice(part * 128, (part + 1) * 128)
            for c in range(4):
                ref[4 * part + c, at, :DH, :] = grad_win[c * DH : (c + 1) * DH, lanes]
                ref[4 * part + c, at, DH:, :] = grad_wout[c * DH // 4 : (c + 1) * DH // 4, lanes]

    def one_head(h):
        rows = pl.ds(pl.multiple_of(h * DH, DH), DH)
        grad_gated = grad_s[rows, :]
        normed = out_norm[rows, :]
        grad_normo = grad_gated * proj[h, :DH, :].astype(F32)
        grad_att = (inv * (grad_normo - first - normed * second)).astype(BF16)
        grads = ([], [], [])
        for i in range(2):
            low = i * SLOT
            lanes = slice(low, low + SLOT)
            value = proj[h, DH : 2 * DH, lanes]
            query = proj[h, 2 * DH : 3 * DH, lanes] * BF16(0.5 * DH**-0.5)
            key = proj[h, 3 * DH :, lanes] * BF16(0.5 * DH**-0.5)
            grad = grad_att[:, lanes]
            scores = tn(value[:, :TILE], grad) * score_slopes[h, i, :, :SLOT].astype(F32)
            scores = scores.astype(BF16)
            tail = tn(value[:, TILE:], grad[:, TILE:]) * score_slopes[h, i, :, SLOT:].astype(F32)
            tail = tail.astype(BF16)
            grad_query = nn(key[:, :TILE], scores)
            grads[0].append(nt(grad, weights[h, i, :, :SLOT]))
            grads[0].append(nt(grad[:, TILE:], weights[h, i, :, SLOT:]))
            grads[1].append(grad_query[:, :TILE])
            grads[1].append(grad_query[:, TILE:] + nn(key[:, TILE:], tail))
            grads[2].append(nt(query, scores))
            grads[2].append(nt(query[:, TILE:], tail))
        stacked = [grad_gated * normed] + [jnp.concatenate(blocks, axis=1) for blocks in grads]
        grad_pre = (jnp.concatenate(stacked, axis=0) * slopes[h].astype(F32)).astype(BF16)
        gpre_s[h] = grad_pre
        return nt(grad_pre, xn[...]).astype(BF16), gwo_s[rows, :]

    def head_step(z, carry):
        store_grad(mine, z, *one_head(2 * z + core))
        store_grad(other, z, *one_head(2 * z + 1 - core))
        return carry

    lax.fori_loop(0, H // 2, head_step, 0, unroll=True)
    sum_s[...] = tn(win[...].reshape(4 * D, D), gpre_s[...].reshape(4 * D, tokens))
    for i in range(tokens // 128):
        lanes = slice(i * 128, (i + 1) * 128)
        grad = 0.5 * sum_s[:, lanes]
        normed = 2.0 * xn[:, lanes].astype(F32)
        lead = jnp.mean(grad, axis=0, keepdims=True)
        cross = jnp.mean(grad * normed, axis=0, keepdims=True)
        total = gy_s[:, lanes].astype(F32) + inv_in[:, lanes] * (grad - lead - normed * cross)
        here = slice(i % 2 * 128, (i % 2 + 1) * 128)
        gfeat[:, i // 2, :, here] = total.astype(BF16).reshape(H, DH, 128)


def run_forward(place, meta, xa, pieces):
    tokens = 2 * SLOT
    shape = jax.ShapeDtypeStruct
    return pl.pallas_call(
        forward_kernel,
        out_shape=(
            shape((4, 2, DH, SLOT), BF16),
            shape((4, 2, DH, SLOT), BF16),
            shape((H, 4 * DH, D), BF16),
            shape((D, D), BF16),
            shape((D, tokens), BF16),
            shape((1, tokens), F32),
            shape((H, 4 * DH, tokens), BF16),
            shape((H, 4 * DH, tokens), BF16),
            shape((H, 2, TILE, 3 * TILE), BF16),
            shape((H, 2, TILE, 3 * TILE), BF16),
            shape((D, tokens), F32),
            shape((1, tokens), F32),
            shape((D, tokens), BF16),
        ),
        in_specs=[SMEM, SMEM] + [VMEM] * 9,
        out_specs=(VMEM,) * 13,
        scratch_shapes=[pltpu.VMEM((H, 2, DH, SLOT), BF16), pltpu.VMEM((D, tokens), F32)],
        compiler_params=params(14),
        cost_estimate=cost(10**10, 2**24),
    )(place, meta, xa, *pieces)


def run_backward(place, meta, grad_y, saved):
    tokens = 2 * SLOT
    piece = jax.ShapeDtypeStruct((16, 4, PIECE, 128), BF16)
    return pl.pallas_call(
        backward_kernel,
        out_shape=(jax.ShapeDtypeStruct((H, 2, DH, SLOT), BF16), piece, piece),
        in_specs=[SMEM, SMEM] + [VMEM] * 12,
        out_specs=(VMEM,) * 3,
        cost_estimate=cost(12 * 10**9, 2**24),
        scratch_shapes=[
            pltpu.VMEM((D, tokens), F32),
            pltpu.VMEM((D, tokens), BF16),
            pltpu.VMEM((H, 4 * DH, tokens), BF16),
            pltpu.VMEM((D, tokens), F32),
            pltpu.VMEM((D, D), BF16),
        ],
        compiler_params=params(14),
    )(place, meta, grad_y, *saved)


def finish_kernel(arrived, grad_in, grad_out):
    factor = float(HIST * 32 * SLOT) ** -0.5
    for part in range(4):
        lanes = slice(part * 128, (part + 1) * 128)
        for c in range(4):
            block = arrived[4 * part + c].astype(F32) * factor
            grad_in[c, :, lanes] = block[:DH]
            grad_out[c * DH // 4 : (c + 1) * DH // 4, lanes] = block[DH:]


def shift(x, axis, k):
    return lax.ppermute(x, axis, [(i, (i + k) % 4) for i in range(4)])


def trade(x, axis):
    return lax.ppermute(x, axis, [(0, 1), (1, 0)])


def turn(part, k, flip):
    pairs = []
    for y in range(4):
        for x in range(4):
            for core in range(2):
                goal = 4 * y + (x + k) % 4 if core == flip else 4 * ((y + k) % 4) + x
                pairs.append(((4 * y + x) * 2 + core, goal * 2 + core))
    return lax.ppermute(part, ("y", "x", "core"), pairs)


def gather_weights(shards):
    own = [jnp.stack(shards)]
    own += [turn(own[0], k, 0) for k in range(1, 4)]
    return own + [trade(part, "core") for part in own]


def swap(x, axes):
    return lax.all_to_all(x, axes, split_axis=0, concat_axis=0, tiled=True)


def on_device(features, cotangent, lengths, route, w_in, w_out):
    groups = lax.axis_size(DP)
    col = lax.axis_index(COL)
    core = lax.axis_index("core")
    zhi = lax.axis_index("zhi")
    route = route.T
    x = lax.axis_index("x")
    y = lax.axis_index("y")
    along = jnp.where(core == 0, x, y)
    place = jnp.stack([col, core, zhi, along, x + y - along]).astype(jnp.int32)

    sent, piece = pl.pallas_call(
        spread_kernel,
        out_shape=(
            jax.ShapeDtypeStruct((groups, 2 * DH + META, TILE), BF16),
            jax.ShapeDtypeStruct((PIECE, D), BF16),
        ),
        in_specs=[SMEM, SMEM, ANY, ANY, ANY],
        out_specs=(VMEM, VMEM),
        scratch_shapes=[pltpu.VMEM((HIST, DH, SLOT), BF16), pltpu.SemaphoreType.DMA((3,))],
        compiler_params=params(60),
    )(route, lengths, features, w_in.transpose(0, 2, 1), w_out)
    arrived = swap(sent, DP)
    shards = [piece] + [shift(piece, "zhi", k) for k in range(1, 4)]
    rows, meta = pl.pallas_call(
        settle_kernel,
        out_shape=(
            jax.ShapeDtypeStruct((HIST, DH, SLOT), BF16),
            jax.ShapeDtypeStruct((2, HIST), jnp.int32),
        ),
        in_specs=[VMEM, ANY, ANY, ANY],
        out_specs=(VMEM, SMEM),
        compiler_params=params(14),
    )(arrived, *shards[1:])
    pieces = gather_weights(shards)
    xa = swap(rows, COL).reshape(H, 2, DH, SLOT)
    grad_y = lax.dynamic_slice_in_dim(cotangent, 2 * col, 2, 0)
    msame, mcross, *saved = run_forward(place, meta, xa, pieces)
    gfeat, mine, other = run_backward(place, meta, grad_y, saved)
    home = swap(gfeat.reshape(HIST, DH, SLOT), COL)

    def local(kernel, outs, *args):
        return pl.pallas_call(
            kernel,
            out_shape=outs,
            in_specs=[SMEM] + [VMEM] * (len(args) - 1),
            out_specs=(VMEM,) * len(outs),
            compiler_params=params(14),
        )(*args)

    part = jax.ShapeDtypeStruct((4, 4, PIECE, 128), BF16)
    sums = local(add_kernel, (part,) * 4, place, mine, trade(other, "core"))
    came = [turn(sums[k], k, 0) for k in range(1, 4)]
    part = jax.ShapeDtypeStruct((4, PIECE, 128), BF16)
    sums = local(cross_kernel, (part,) * 4, place, sums[0], *came)
    gate1 = sums[1]
    came = [turn(sums[k], k, 1) for k in range(1, 4)]
    part = jax.ShapeDtypeStruct((PIECE, 128), BF16)
    kept = jax.ShapeDtypeStruct((PIECE, 128), F32)
    sums = local(depth_kernel, (kept,) + (part,) * 3, place, sums[0], *came)
    gate2 = sums[1]
    came = [shift(sums[k], "zhi", k) for k in range(1, 4)]
    total, rounded = pl.pallas_call(
        last_kernel,
        out_shape=(kept, part),
        in_specs=[VMEM] * 4,
        out_specs=(VMEM, VMEM),
        compiler_params=params(14),
    )(sums[0], *came)

    def col_pairs(same, cross, after):
        pair = jax.ShapeDtypeStruct((2, 2, DH, SLOT), BF16)
        pairs = pl.pallas_call(
            pair_kernel,
            out_shape=(pair,) * 4,
            in_specs=[VMEM, VMEM, ANY],
            out_specs=(VMEM,) * 4,
            compiler_params=params(14),
        )(same, trade(cross, "core"), after)
        return [pairs[0]] + [shift(pairs[k], "zhi", k) for k in range(1, 4)]

    back = pl.pallas_call(
        return_kernel,
        out_shape=jax.ShapeDtypeStruct((groups, DH, SLOT), BF16),
        in_specs=[SMEM, VMEM, ANY],
        out_specs=VMEM,
        compiler_params=params(14),
    )(meta, home, gate2)
    arrived = swap(back, DP)
    moved = col_pairs(msame, mcross, rounded)
    block = jax.ShapeDtypeStruct((HIST, DH, SLOT), BF16)
    grad_features = pl.pallas_call(
        collect_kernel,
        out_shape=block,
        in_specs=[SMEM, VMEM],
        out_specs=VMEM,
        compiler_params=params(14),
    )(route, arrived)
    mixed = pl.pallas_call(
        mixed_kernel,
        out_shape=block,
        in_specs=[SMEM] + [VMEM] * 4,
        out_specs=VMEM,
        compiler_params=params(14),
    )(place, *moved)

    whole = pl.pallas_call(
        repeat_kernel,
        out_shape=jax.ShapeDtypeStruct((16, PIECE, 128), BF16),
        in_specs=[VMEM, VMEM, ANY],
        out_specs=VMEM,
        compiler_params=params(14),
    )(total, trade(rounded, "zlo"), arrived)
    whole = swap(whole, ("y", "x"))
    grad_in, grad_out = pl.pallas_call(
        finish_kernel,
        out_shape=(jax.ShapeDtypeStruct((4, DH, D), F32), jax.ShapeDtypeStruct((DH, D), F32)),
        in_specs=[VMEM],
        out_specs=(VMEM, VMEM),
        compiler_params=params(14),
    )(whole)
    return (mixed, grad_features, grad_in.transpose(0, 2, 1), grad_out)


def solution(mesh):
    split = Mesh(mesh.devices.reshape(4, 4, 2, 4, 2), ("y", "x", "zlo", "zhi", "core"))
    in_specs = (P(DP, COL, None), P(DP, None, None), P(DP), P(DP, None), P(None, None, COL), P(COL, None))
    out_specs = (P(DP, COL, None), P(DP, COL, None), P(None, None, COL), P(COL, None))
    return jax.shard_map(
        on_device, mesh=split, in_specs=in_specs, out_specs=out_specs, check_vma=False
    )
```

```python
import jax
import jax.numpy as jnp
from jax import lax
from jax.experimental import pallas as pl
from jax.experimental.pallas import tpu as pltpu
from jax.sharding import Mesh
from jax.sharding import PartitionSpec as P

D = 512
H = 8
DH = 64
SLOT = 256
HIST = 16
EPS = 1e-05
META = 16
TILE = 128
ROWS = 5 * DH
PIECE = ROWS // 4
F32 = jnp.float32
BF16 = jnp.bfloat16
DP = ("y", "x", "zlo")
COL = ("zhi", "core")
VMEM = pl.BlockSpec(memory_space=pltpu.VMEM)
SMEM = pl.BlockSpec(memory_space=pltpu.SMEM)
ANY = pl.BlockSpec(memory_space=pl.ANY)


def params(mib):
    return pltpu.CompilerParams(vmem_limit_bytes=mib * 1024 * 1024)


def cost(flops, moved):
    return pl.CostEstimate(flops=flops, bytes_accessed=moved, transcendentals=0)


def spread_kernel(route, lengths, rows, proj, wout, sent, piece, rows_s, sems):
    along = jnp.where(lax.axis_index("core") == 0, lax.axis_index("x"), lax.axis_index("y"))
    wrows = pl.ds(pl.multiple_of(along * (DH // 4), DH // 4), DH // 4)
    copies = (
        pltpu.make_async_copy(proj.at[along], piece.at[pl.ds(0, DH)], sems.at[0]),
        pltpu.make_async_copy(wout.at[wrows], piece.at[pl.ds(DH, DH // 4)], sems.at[1]),
        pltpu.make_async_copy(rows, rows_s, sems.at[2]),
    )
    for copy in copies:
        copy.start()
    sent[...] = jnp.zeros_like(sent)
    for copy in copies:
        copy.wait()
    for h in range(HIST):
        group = route[0, h]
        sent[group, :DH, :] = rows_s[h, :, :TILE]
        sent[group, DH : 2 * DH, :] = rows_s[h, :, TILE:]
        slot = (route[1, h] + 1).astype(F32)
        count = lengths[h].astype(F32)
        note = jnp.concatenate([jnp.full((8, TILE), slot, F32), jnp.full((8, TILE), count, F32)], axis=0)
        sent[group, 2 * DH :, :] = note.astype(BF16)


def settle_kernel(arrived, shard1, shard2, shard3, rows, meta):
    codes = []
    for group in range(arrived.shape[0]):
        note = arrived[group, 2 * DH :, :].astype(F32)
        code = jnp.max(note[:8] * 512.0 + note[8:])
        codes.append(code.astype(jnp.int32))
    for group, code in enumerate(codes):

        @pl.when(code >= 512)
        def _():
            slot = lax.shift_right_logical(code, 9) - 1
            rows[slot, :, :TILE] = arrived[group, :DH, :]
            rows[slot, :, TILE:] = arrived[group, DH : 2 * DH, :]
            meta[0, slot] = group
            meta[1, slot] = code & 511


def add_kernel(place, mine, came, sum0, sum1, sum2, sum3):
    core = place[1]
    for k, total in enumerate((sum0, sum1, sum2, sum3)):
        ahead = lax.rem(place[3] + k, 4)
        for j in range(4):
            piece = jnp.where(core == 0, 4 * j + ahead, 4 * ahead + j)
            total[j] = (mine[piece].astype(F32) + came[piece].astype(F32)).astype(BF16)


def cross_kernel(place, kept, came1, came2, came3, sum0, sum1, sum2, sum3):
    for k, total in enumerate((sum0, sum1, sum2, sum3)):
        j = lax.rem(place[4] + k, 4)
        part = kept[j].astype(F32)
        for came in (came1, came2, came3):
            part = part + came[j].astype(F32)
        total[...] = part.astype(BF16)


def depth_kernel(place, kept, came1, came2, came3, sum0, sum1, sum2, sum3):
    for k, total in enumerate((sum0, sum1, sum2, sum3)):
        z = lax.rem(place[2] + k, 4)
        part = kept[z].astype(F32)
        for came in (came1, came2, came3):
            part = part + came[z].astype(F32)
        total[...] = part.astype(BF16) if k else part


def last_kernel(kept, came1, came2, came3, total, rounded):
    part = kept[...]
    for came in (came1, came2, came3):
        part = part + came[...].astype(F32)
    total[...] = part
    rounded[...] = part.astype(BF16)


def repeat_kernel(total, came, after, whole):
    summed = (total[...] + came[...].astype(F32)).astype(BF16)
    for group in range(whole.shape[0]):
        whole[group] = summed


def pair_kernel(same, came, after, pair0, pair1, pair2, pair3):
    for k, pair in enumerate((pair0, pair1, pair2, pair3)):
        pair[0] = same[k]
        pair[1] = came[k]


def return_kernel(meta, rows, after, sent):
    sent[...] = jnp.zeros_like(sent)
    for k in range(HIST):
        sent[meta[0, k]] = rows[k]


def collect_kernel(route, arrived, rows, done):
    done[...] = jnp.zeros_like(done)
    for h in range(HIST):
        rows[h] = arrived[route[0, h]]


def mixed_kernel(place, pair0, pair1, pair2, pair3, after1, after2, mixed):
    core = place[1]
    for k, pair in enumerate((pair0, pair1, pair2, pair3)):
        for side in range(2):
            owner = 2 * wrap(place[2], k) + (core if side == 0 else 1 - core)
            for i in range(2):
                mixed[2 * owner + i] = pair[side, i]


def tn(a, b):
    return lax.dot_general(a, b, (((0,), (0,)), ((), ())), preferred_element_type=F32)


def nt(a, b):
    return lax.dot_general(a, b, (((1,), (1,)), ((), ())), preferred_element_type=F32)


def nn(a, b):
    return lax.dot_general(a, b, (((1,), (0,)), ((), ())), preferred_element_type=F32)


def silu_parts(half):
    t = jnp.tanh(half)
    up = 1.0 + t
    silu = half * up
    return silu, up + silu * (1.0 - t)


def live_row(meta, col):
    at = lax.broadcasted_iota(jnp.int32, (1, SLOT), 1)
    rows = [(at < meta[1, 2 * col + i]).astype(F32) for i in range(2)]
    return jnp.concatenate(rows, axis=1)


def wrap(position, back):
    return lax.rem(position - back + 4, 4)


def split_chunks(place, chunks, same, cross):
    for k in range(4):
        goal = 2 * lax.rem(place[2] + k, 4)
        same[k] = chunks[goal + place[1]]
        cross[k] = chunks[goal + 1 - place[1]]


def forward_kernel(
    place,
    meta,
    xa,
    own0,
    own1,
    own2,
    own3,
    far0,
    far1,
    far2,
    far3,
    msame,
    mcross,
    win,
    wout,
    xn,
    inv_in,
    slopes,
    proj,
    weights,
    score_slopes,
    out_norm,
    inv_out,
    gated,
    mixed,
    x_s,
):
    tokens = 2 * SLOT
    col = place[0]
    core = place[1]
    for i in range(2):
        x_s[:, i * SLOT : (i + 1) * SLOT] = xa[:, i].reshape(D, SLOT).astype(F32)
    for side, refs, along in ((core, (own0, own1, own2, own3), place[3]), (1 - core, (far0, far1, far2, far3), place[4])):
        for k in range(4):
            piece = wrap(along, k)
            for z in range(4):
                head = 2 * wrap(place[2], z) + side
                at = pl.multiple_of(piece * DH, DH)
                win[head, pl.ds(at, DH), :] = refs[k][z, :DH, :]
                at = pl.multiple_of(head * DH + piece * (DH // 4), DH // 4)
                wout[pl.ds(at, DH // 4), :] = refs[k][z, DH:, :]

    for i in range(tokens // 128):
        lanes = slice(i * 128, (i + 1) * 128)
        x = x_s[:, lanes]
        centred = x - jnp.mean(x, axis=0, keepdims=True)
        inv = lax.rsqrt(jnp.mean(centred * centred, axis=0, keepdims=True) + EPS)
        inv_in[:, lanes] = inv
        xn[:, lanes] = (0.5 * (centred * inv)).astype(BF16)

    live = live_row(meta, col)
    square = (TILE, TILE)
    causal = lax.broadcasted_iota(jnp.int32, square, 0) <= lax.broadcasted_iota(jnp.int32, square, 1)

    def one_head(h):
        silu, slope = silu_parts(nn(win[h], xn[...]))
        slopes[h] = slope.astype(BF16)
        rounded = silu.astype(BF16)
        proj[h] = rounded
        scores = []
        for i in range(2):
            low = i * SLOT
            key = rounded[3 * DH :, low : low + SLOT] * BF16(0.5 * DH**-0.5)
            query = rounded[2 * DH : 3 * DH, low : low + SLOT]
            both = tn(key[:, :TILE], query)
            scores.append((both[:, :TILE], both[:, TILE:], tn(key[:, TILE:], query[:, TILE:])))
        parts = []
        for i in range(2):
            low = i * SLOT
            value = rounded[DH : 2 * DH, low : low + SLOT]
            held = []
            for at, half in enumerate(scores[i]):
                weight, slope = silu_parts(half)
                if at != 1:
                    weight = jnp.where(causal, weight, 0.0)
                    slope = jnp.where(causal, slope, 0.0)
                lanes = slice(at * TILE, (at + 1) * TILE)
                held.append(weight.astype(BF16))
                weights[h, i, :, lanes] = held[at]
                score_slopes[h, i, :, lanes] = slope.astype(BF16)
            first = nn(value[:, :TILE], jnp.concatenate(held[:2], axis=1))
            parts += [first[:, :TILE], first[:, TILE:] + nn(value[:, TILE:], held[2])]
        att = jnp.concatenate(parts, axis=1) * live
        out_norm[pl.ds(pl.multiple_of(h * DH, DH), DH), :] = att
        return att

    def head_step(z, sums):
        for h in (2 * z, 2 * z + 1):
            att = one_head(h)
            sums = (
                sums[0] + jnp.sum(att, axis=0, keepdims=True),
                sums[1] + jnp.sum(att * att, axis=0, keepdims=True),
            )
        return sums

    zero = jnp.zeros((1, tokens), F32)
    totals, squares = lax.fori_loop(0, H // 2, head_step, (zero, zero), unroll=True)
    mean = totals / D
    inv = lax.rsqrt(squares / D - mean * mean + EPS)
    inv_out[...] = inv

    def gate_step(h, carry):
        rows = pl.ds(h * DH, DH)
        normed = (out_norm[rows, :] - mean) * inv
        out_norm[rows, :] = normed
        gated[rows, :] = (normed * proj[h, :DH, :].astype(F32)).astype(BF16)
        return carry

    lax.fori_loop(0, H, gate_step, 0, unroll=4)
    out = (x_s[...] + tn(wout[...], gated[...])).astype(BF16)
    for i in range(2):
        mixed[:, i] = out[:, i * SLOT : (i + 1) * SLOT].reshape(H, DH, SLOT)
    split_chunks(place, mixed, msame, mcross)


def backward_kernel(
    place,
    meta,
    gy_ref,
    win,
    wout,
    xn,
    inv_in,
    slopes,
    proj,
    weights,
    score_slopes,
    out_norm,
    inv_out,
    gated,
    gfeat,
    mine,
    other,
    grad_s,
    gy_s,
    gpre_s,
    sum_s,
    gwo_s,
):
    tokens = 2 * SLOT
    core = place[1]
    for i in range(2):
        gy_s[:, i * SLOT : (i + 1) * SLOT] = gy_ref[i]
    grad_s[...] = nn(wout[...], gy_s[...])
    gwo_s[...] = nt(gated[...], gy_s[...]).astype(BF16)

    def sum_step(h, sums):
        rows = pl.ds(h * DH, DH)
        grad = grad_s[rows, :] * proj[h, :DH, :].astype(F32)
        return (
            sums[0] + jnp.sum(grad, axis=0, keepdims=True),
            sums[1] + jnp.sum(grad * out_norm[rows, :], axis=0, keepdims=True),
        )

    zero = jnp.zeros((1, tokens), F32)
    first, second = lax.fori_loop(0, H, sum_step, (zero, zero), unroll=4)
    first = first / D
    second = second / D
    inv = inv_out[...] * live_row(meta, place[0])

    def store_grad(ref, at, grad_win, grad_wout):
        for part in range(4):
            lanes = slice(part * 128, (part + 1) * 128)
            for c in range(4):
                ref[4 * part + c, at, :DH, :] = grad_win[c * DH : (c + 1) * DH, lanes]
                ref[4 * part + c, at, DH:, :] = grad_wout[c * DH // 4 : (c + 1) * DH // 4, lanes]

    def one_head(h):
        rows = pl.ds(pl.multiple_of(h * DH, DH), DH)
        grad_gated = grad_s[rows, :]
        normed = out_norm[rows, :]
        grad_normo = grad_gated * proj[h, :DH, :].astype(F32)
        grad_att = (inv * (grad_normo - first - normed * second)).astype(BF16)
        grads = ([], [], [])
        for i in range(2):
            low = i * SLOT
            lanes = slice(low, low + SLOT)
            value = proj[h, DH : 2 * DH, lanes]
            query = proj[h, 2 * DH : 3 * DH, lanes] * BF16(0.5 * DH**-0.5)
            key = proj[h, 3 * DH :, lanes] * BF16(0.5 * DH**-0.5)
            grad = grad_att[:, lanes]
            scores = tn(value[:, :TILE], grad) * score_slopes[h, i, :, :SLOT].astype(F32)
            scores = scores.astype(BF16)
            tail = tn(value[:, TILE:], grad[:, TILE:]) * score_slopes[h, i, :, SLOT:].astype(F32)
            tail = tail.astype(BF16)
            grad_query = nn(key[:, :TILE], scores)
            grads[0].append(nt(grad, weights[h, i, :, :SLOT]))
            grads[0].append(nt(grad[:, TILE:], weights[h, i, :, SLOT:]))
            grads[1].append(grad_query[:, :TILE])
            grads[1].append(grad_query[:, TILE:] + nn(key[:, TILE:], tail))
            grads[2].append(nt(query, scores))
            grads[2].append(nt(query[:, TILE:], tail))
        stacked = [grad_gated * normed] + [jnp.concatenate(blocks, axis=1) for blocks in grads]
        grad_pre = (jnp.concatenate(stacked, axis=0) * slopes[h].astype(F32)).astype(BF16)
        gpre_s[h] = grad_pre
        return nt(grad_pre, xn[...]).astype(BF16), gwo_s[rows, :]

    def head_step(z, carry):
        store_grad(mine, z, *one_head(2 * z + core))
        store_grad(other, z, *one_head(2 * z + 1 - core))
        return carry

    lax.fori_loop(0, H // 2, head_step, 0, unroll=True)
    sum_s[...] = tn(win[...].reshape(4 * D, D), gpre_s[...].reshape(4 * D, tokens))
    for i in range(tokens // 128):
        lanes = slice(i * 128, (i + 1) * 128)
        grad = 0.5 * sum_s[:, lanes]
        normed = 2.0 * xn[:, lanes].astype(F32)
        lead = jnp.mean(grad, axis=0, keepdims=True)
        cross = jnp.mean(grad * normed, axis=0, keepdims=True)
        total = gy_s[:, lanes].astype(F32) + inv_in[:, lanes] * (grad - lead - normed * cross)
        here = slice(i % 2 * 128, (i % 2 + 1) * 128)
        gfeat[:, i // 2, :, here] = total.astype(BF16).reshape(H, DH, 128)


def run_forward(place, meta, xa, pieces):
    tokens = 2 * SLOT
    shape = jax.ShapeDtypeStruct
    return pl.pallas_call(
        forward_kernel,
        out_shape=(
            shape((4, 2, DH, SLOT), BF16),
            shape((4, 2, DH, SLOT), BF16),
            shape((H, 4 * DH, D), BF16),
            shape((D, D), BF16),
            shape((D, tokens), BF16),
            shape((1, tokens), F32),
            shape((H, 4 * DH, tokens), BF16),
            shape((H, 4 * DH, tokens), BF16),
            shape((H, 2, TILE, 3 * TILE), BF16),
            shape((H, 2, TILE, 3 * TILE), BF16),
            shape((D, tokens), F32),
            shape((1, tokens), F32),
            shape((D, tokens), BF16),
        ),
        in_specs=[SMEM, SMEM] + [VMEM] * 9,
        out_specs=(VMEM,) * 13,
        scratch_shapes=[pltpu.VMEM((H, 2, DH, SLOT), BF16), pltpu.VMEM((D, tokens), F32)],
        compiler_params=params(14),
        cost_estimate=cost(10**10, 2**24),
    )(place, meta, xa, *pieces)


def run_backward(place, meta, grad_y, saved):
    tokens = 2 * SLOT
    piece = jax.ShapeDtypeStruct((16, 4, PIECE, 128), BF16)
    return pl.pallas_call(
        backward_kernel,
        out_shape=(jax.ShapeDtypeStruct((H, 2, DH, SLOT), BF16), piece, piece),
        in_specs=[SMEM, SMEM] + [VMEM] * 12,
        out_specs=(VMEM,) * 3,
        cost_estimate=cost(12 * 10**9, 2**24),
        scratch_shapes=[
            pltpu.VMEM((D, tokens), F32),
            pltpu.VMEM((D, tokens), BF16),
            pltpu.VMEM((H, 4 * DH, tokens), BF16),
            pltpu.VMEM((D, tokens), F32),
            pltpu.VMEM((D, D), BF16),
        ],
        compiler_params=params(14),
    )(place, meta, grad_y, *saved)


def finish_kernel(arrived, grad_in, grad_out, done):
    done[...] = jnp.zeros_like(done)
    factor = float(HIST * 32 * SLOT) ** -0.5
    for part in range(4):
        lanes = slice(part * 128, (part + 1) * 128)
        for c in range(4):
            block = arrived[4 * part + c].astype(F32) * factor
            grad_in[c, :, lanes] = block[:DH]
            grad_out[c * DH // 4 : (c + 1) * DH // 4, lanes] = block[DH:]


def shift(x, axis, k):
    return lax.ppermute(x, axis, [(i, (i + k) % 4) for i in range(4)])


def trade(x, axis):
    return lax.ppermute(x, axis, [(0, 1), (1, 0)])


def turn(part, k, flip):
    pairs = []
    for y in range(4):
        for x in range(4):
            for core in range(2):
                goal = 4 * y + (x + k) % 4 if core == flip else 4 * ((y + k) % 4) + x
                pairs.append(((4 * y + x) * 2 + core, goal * 2 + core))
    return lax.ppermute(part, ("y", "x", "core"), pairs)


def gather_weights(shards):
    own = [jnp.stack(shards)]
    own += [turn(own[0], k, 0) for k in range(1, 4)]
    return own + [trade(part, "core") for part in own]


def swap(x, axes):
    return lax.all_to_all(x, axes, split_axis=0, concat_axis=0, tiled=True)


def on_device(features, cotangent, lengths, route, w_in, w_out):
    groups = lax.axis_size(DP)
    col = lax.axis_index(COL)
    core = lax.axis_index("core")
    zhi = lax.axis_index("zhi")
    route = route.T
    x = lax.axis_index("x")
    y = lax.axis_index("y")
    along = jnp.where(core == 0, x, y)
    place = jnp.stack([col, core, zhi, along, x + y - along]).astype(jnp.int32)

    sent, piece = pl.pallas_call(
        spread_kernel,
        out_shape=(
            jax.ShapeDtypeStruct((groups, 2 * DH + META, TILE), BF16),
            jax.ShapeDtypeStruct((PIECE, D), BF16),
        ),
        in_specs=[SMEM, SMEM, ANY, ANY, ANY],
        out_specs=(VMEM, VMEM),
        scratch_shapes=[pltpu.VMEM((HIST, DH, SLOT), BF16), pltpu.SemaphoreType.DMA((3,))],
        compiler_params=params(60),
    )(route, lengths, features, w_in.transpose(0, 2, 1), w_out)
    arrived = swap(sent, DP)
    shards = [piece] + [shift(piece, "zhi", k) for k in range(1, 4)]
    rows, meta = pl.pallas_call(
        settle_kernel,
        out_shape=(
            jax.ShapeDtypeStruct((HIST, DH, SLOT), BF16),
            jax.ShapeDtypeStruct((2, HIST), jnp.int32),
        ),
        in_specs=[VMEM, ANY, ANY, ANY],
        out_specs=(VMEM, SMEM),
        compiler_params=params(14),
    )(arrived, *shards[1:])
    pieces = gather_weights(shards)
    xa = swap(rows, COL).reshape(H, 2, DH, SLOT)
    grad_y = lax.dynamic_slice_in_dim(cotangent, 2 * col, 2, 0)
    msame, mcross, *saved = run_forward(place, meta, xa, pieces)
    gfeat, mine, other = run_backward(place, meta, grad_y, saved)
    home = swap(gfeat.reshape(HIST, DH, SLOT), COL)

    def local(kernel, outs, *args):
        return pl.pallas_call(
            kernel,
            out_shape=outs,
            in_specs=[SMEM] + [VMEM] * (len(args) - 1),
            out_specs=(VMEM,) * len(outs),
            compiler_params=params(14),
        )(*args)

    part = jax.ShapeDtypeStruct((4, 4, PIECE, 128), BF16)
    sums = local(add_kernel, (part,) * 4, place, mine, trade(other, "core"))
    came = [turn(sums[k], k, 0) for k in range(1, 4)]
    part = jax.ShapeDtypeStruct((4, PIECE, 128), BF16)
    sums = local(cross_kernel, (part,) * 4, place, sums[0], *came)
    gate1 = sums[1]
    came = [turn(sums[k], k, 1) for k in range(1, 4)]
    part = jax.ShapeDtypeStruct((PIECE, 128), BF16)
    kept = jax.ShapeDtypeStruct((PIECE, 128), F32)
    sums = local(depth_kernel, (kept,) + (part,) * 3, place, sums[0], *came)
    gate2 = sums[1]
    came = [shift(sums[k], "zhi", k) for k in range(1, 4)]
    total, rounded = pl.pallas_call(
        last_kernel,
        out_shape=(kept, part),
        in_specs=[VMEM] * 4,
        out_specs=(VMEM, VMEM),
        compiler_params=params(14),
    )(sums[0], *came)

    def col_pairs(same, cross, after):
        pair = jax.ShapeDtypeStruct((2, 2, DH, SLOT), BF16)
        pairs = pl.pallas_call(
            pair_kernel,
            out_shape=(pair,) * 4,
            in_specs=[VMEM, VMEM, ANY],
            out_specs=(VMEM,) * 4,
            compiler_params=params(14),
        )(same, trade(cross, "core"), after)
        return [pairs[0]] + [shift(pairs[k], "zhi", k) for k in range(1, 4)]

    back = pl.pallas_call(
        return_kernel,
        out_shape=jax.ShapeDtypeStruct((groups, DH, SLOT), BF16),
        in_specs=[SMEM, VMEM, ANY],
        out_specs=VMEM,
        compiler_params=params(14),
    )(meta, home, gate2)
    arrived = swap(back, DP)
    moved = col_pairs(msame, mcross, rounded)
    block = jax.ShapeDtypeStruct((HIST, DH, SLOT), BF16)
    token = jax.ShapeDtypeStruct((8, 128), F32)
    grad_features, done1 = pl.pallas_call(
        collect_kernel,
        out_shape=(block, token),
        in_specs=[SMEM, VMEM],
        out_specs=(VMEM, VMEM),
        compiler_params=params(14),
    )(route, arrived)
    whole = pl.pallas_call(
        repeat_kernel,
        out_shape=jax.ShapeDtypeStruct((16, PIECE, 128), BF16),
        in_specs=[VMEM, VMEM, ANY],
        out_specs=VMEM,
        compiler_params=params(14),
    )(total, trade(rounded, "zlo"), arrived)
    whole = swap(whole, ("y", "x"))
    grad_in, grad_out, done2 = pl.pallas_call(
        finish_kernel,
        out_shape=(jax.ShapeDtypeStruct((4, DH, D), F32), jax.ShapeDtypeStruct((DH, D), F32), token),
        in_specs=[VMEM],
        out_specs=(VMEM, VMEM, VMEM),
        compiler_params=params(14),
    )(whole)
    mixed = pl.pallas_call(
        mixed_kernel,
        out_shape=block,
        in_specs=[SMEM] + [VMEM] * 4 + [ANY] * 2,
        out_specs=VMEM,
        compiler_params=params(14),
    )(place, *moved, done1, done2)
    return (mixed, grad_features, grad_in.transpose(0, 2, 1), grad_out)


def solution(mesh):
    split = Mesh(mesh.devices.reshape(4, 4, 2, 4, 2), ("y", "x", "zlo", "zhi", "core"))
    in_specs = (P(DP, COL, None), P(DP, None, None), P(DP), P(DP, None), P(None, None, COL), P(COL, None))
    out_specs = (P(DP, COL, None), P(DP, COL, None), P(None, None, COL), P(COL, None))
    return jax.shard_map(
        on_device, mesh=split, in_specs=in_specs, out_specs=out_specs, check_vma=False
    )
```
